1024 devices in a mesh: brick: 64 (over x, y), row: 16 (over z, core).
Axes of the slice: x: 8, y: 8, z: 8, core: 2. Of those that a mesh axis runs over, the one named last changes fastest.
Arguments:
- flow_state: float32 [5, 256, 128, 128], P(None, 'brick', 'row'), may hold values from -1.2 to 3.5, as said below
- point_cell: int32 [16384, 64], P(('brick', 'row')), may hold values from 0 to 4095
- normals: float32 [3, 16384, 64], P(None, ('brick', 'row')), may hold values from -4 to 4
- rbf_weights: bfloat16 [16384, 64, 128], P(('brick', 'row')), may hold values from -0.75 to 0.75
- block_owner: int32 [16384, 1], P(('brick', 'row')), may hold values from 0 to 15; in each aligned block of 16 rows (0 to 15, 16 to 31, ...) at most 2 rows name the same one
- block_start: int32 [16384], P(('brick', 'row')), may hold values from 0 to 3968
- stiff_diag: float32 [128, 512], P('row'), may hold values from 0.05 to 0.5
- stiff_chord: float32 [128, 512], P('row'), may hold values from 0.3 to 3
Outputs:
- fluid_next: float32 [5, 256, 128, 128], P(None, 'brick', 'row')
- displacement: float32 [3, 128, 512], P(None, 'row')
- residual: float32 [3, 128, 512], P(None, 'row')
The draws below stay inside these ranges and needn't reach their ends.
Inputs may be any that keep to these rules, and one draw needn't show every extreme that they name: `flow_state`: density (component 0) lies in 0.8 to 1.25, momenta in -1.2 to 1.2, energy in 1.6 to 3.5. `point_cell`: a cell of the device that holds the block. `block_owner`: of the 16 blocks of one device, at most 2 name the same owner. `block_start`: a node of the owner's 4096 nodes such that the window of 128 nodes stays within them.
All inputs are finite; a program needn't handle non-finite values.
Results may differ from the reference program's by a relative error of at most 0.003.
Values sent between devices are 32-bit elements; how exact they have to be, the bound alone decides.
A program may use at most 32 MiB of HBM per device.

```python
import math
import jax
import jax.numpy as jnp
import numpy as np
from jax import lax

CX = 4
CY = 8
CZ = 128
NBLK = 16
BP = 64
BW = 128
SR_DEV = 8
CHORD = 512
ITERS = 3
CAP = 2
NX = 256
NY = 128
BLOCKS = 16384
NODES_DEV = 4096
SROWS = 128
N_BRICK = 64
N_ROW = 16


def draw_flow_state(key, part):
    key = jax.random.fold_in(key, 11)
    keys = jax.random.split(key, 3)
    shape = (NX, NY, CZ)
    density = jax.random.uniform(keys[0], shape, jnp.float32, 0.8, 1.25)
    momenta = jnp.clip(0.3 * jax.random.normal(keys[1], (3,) + shape, jnp.float32), -1.2, 1.2)
    energy = jnp.clip(2.5 + 0.3 * jax.random.normal(keys[2], shape, jnp.float32), 1.6, 3.5)
    return jnp.concatenate([density[None], momenta, energy[None]], axis=0)


def place_ends(entries, rng, low, top_value):
    index_at = [jax.random.randint(jax.random.fold_in(rng, axis), (), 0, length) for axis, length in enumerate(entries.shape)]
    longest = entries.shape.index(max(entries.shape))
    neighbour = index_at[:longest] + [(index_at[longest] + 1) % entries.shape[longest]] + index_at[longest + 1:]
    return entries.at[tuple(index_at)].set(low).at[tuple(neighbour)].set(top_value)


def block_levels(stream_key, extent, cuts, low, high):
    loudness, own = 1.0, jax.random.fold_in(stream_key, 6)
    for axis_at, blocks in cuts:
        heights = jnp.exp(jax.random.uniform(jax.random.fold_in(own, axis_at), (blocks,), jnp.float32, low / len(cuts), high / len(cuts)))
        loudness = loudness * jnp.repeat(heights, extent[axis_at] // blocks).reshape([-1 if axis == axis_at else 1 for axis in range(len(extent))])
    return loudness


def routed_block(stream_key, own, number, rows, amount, top, most, lean):
    order = jax.random.permutation(stream_key, amount)
    heavy_load, common = portions_of(amount, rows * top, most, lean, True), portions_of(amount, rows * top, most, lean, False)
    places = jnp.arange(amount)

    def named(lengths, turn):
        used = int((lengths > 0).sum())
        fixed = max(1, used // 4)
        passed = fixed + (places - fixed + turn * (used - fixed)) % max(1, amount - fixed)
        return jnp.zeros((amount,), jnp.int32).at[order[jnp.where(places < fixed, places, passed)]].set(jnp.asarray(lengths, jnp.int32))

    lengths = jnp.where(number % 4 == 0, named(heavy_load, number // 4), named(common, number - number // 4 - 1))
    mixed = jax.random.permutation(jax.random.fold_in(own, 3), amount)
    source_of, sink = mixed[0:amount // 2 * 2:2], mixed[1:amount // 2 * 2:2]
    slack = jnp.minimum(lengths[source_of] - 1, most - lengths[sink]) // 2
    slack = jnp.where((source_of == order[0]) | (sink == order[0]) | (lengths[sink] == 0), 0, jnp.maximum(slack, 0))
    passed = jax.random.randint(jax.random.fold_in(own, 4), (amount // 2,), 0, 1 << 20) % (slack + 1)
    lengths = lengths.at[source_of].add(-passed).at[sink].add(passed)
    items = jnp.searchsorted(jnp.cumsum(lengths), jnp.arange(rows * top), side="right").astype(jnp.int32)
    table = items.reshape(top, rows).T
    table = table[jax.random.permutation(jax.random.fold_in(own, 1), rows)]
    turn = jax.random.randint(jax.random.fold_in(own, 2), (rows, 1), 0, top)
    return jnp.take_along_axis(table, (jnp.arange(top)[None, :] + turn) % top, axis=1)


def portions_of(number_of, total, limit, lean, full):
    portions = [(1 << 20) // math.isqrt(rank ** lean) + 1 for rank in range(1, number_of + 1)]
    largest = limit if full else min(limit, max(-(-total // number_of), total * portions[0] // sum(portions)))
    least = 1 if total - largest >= number_of - 1 else 0
    counts, surplus = [largest] + [least] * (number_of - 1), total - largest - least * (number_of - 1)
    while surplus > 0:
        candidates = [i for i in range(1, number_of) if counts[i] < largest] or [i for i in range(1, number_of) if counts[i] < limit]
        whole, left = sum([portions[i] for i in candidates]), surplus
        for i in candidates:
            more = min(limit - counts[i], max(1, left * portions[i] // whole), surplus)
            counts[i] = counts[i] + more
            surplus = surplus - more
    return np.array(counts)


def gaussian(own_key, dims, spread, bound, shards=(), held_as=jnp.bfloat16):
    result = jax.random.normal(own_key, dims, jnp.float32) * spread
    if len(shards) > 0:
        result = block_levels(own_key, dims, shards, -0.22, 0.18) * result
    return jnp.clip(result, min=-bound, max=bound).astype(held_as)


def setup_inputs(seed: int = 0) -> dict:
    arg_keys = jax.random.split(jax.random.key(seed), 9)
    flow_state = draw_flow_state(jax.random.fold_in(arg_keys[8], 71), 0)
    point_cell = place_ends(jax.random.randint(arg_keys[1], (BLOCKS, BP), 0, CX * CY * CZ), jax.random.fold_in(arg_keys[1], 1), 0, (CX * CY * CZ) - 1).astype(jnp.int32)
    normals = gaussian(arg_keys[2], (3, BLOCKS, BP), 1.0, 4.0, ((1, 1024),), jnp.float32)
    rbf_weights = gaussian(arg_keys[3], (BLOCKS, BP, BW), BP ** -0.5, 0.75, ((0, 1024),))
    block_owner_keys = jax.random.split(jax.random.fold_in(arg_keys[4], 1), BLOCKS // NBLK)
    block_owner_turns = jax.random.permutation(jax.random.fold_in(arg_keys[4], 3), BLOCKS // NBLK)
    block_owner = jax.vmap(lambda own, number: routed_block(jax.random.fold_in(arg_keys[4], 2), own, number, NBLK, N_ROW, 1, CAP, 2))(block_owner_keys, block_owner_turns).reshape((BLOCKS, 1))
    block_start = place_ends(jax.random.randint(arg_keys[5], (BLOCKS,), 0, NODES_DEV - BW + 1), jax.random.fold_in(arg_keys[5], 1), 0, NODES_DEV - BW).astype(jnp.int32)
    stiff_diag = jnp.clip(jnp.exp(math.log(0.5) - 2.3025851 * jax.random.uniform(arg_keys[6], (SROWS, CHORD), jnp.float32) ** block_levels(arg_keys[6], (SROWS, CHORD), ((0, 16),), -0.2, 0.2)), 0.05, 0.5)
    stiff_chord = jnp.clip(jnp.exp(math.log(3.0) - 2.3025851 * jax.random.uniform(arg_keys[7], (SROWS, CHORD), jnp.float32) ** block_levels(arg_keys[7], (SROWS, CHORD), ((0, 16),), -0.2, 0.2)), 0.3, 3.0)
    return {"flow_state": flow_state, "point_cell": point_cell, "normals": normals, "rbf_weights": rbf_weights, "block_owner": block_owner, "block_start": block_start, "stiff_diag": stiff_diag, "stiff_chord": stiff_chord}


GAMMA_LESS = 0.4
STEP_RATIO = 0.1
SMOOTHING = 0.1


def pressure_of(state):
    density = state[0]
    momenta = state[1:4]
    energy = state[4]
    velocity = momenta / density
    return GAMMA_LESS * (energy - 0.5 * jnp.sum(momenta * velocity, axis=0))


def flux_along(state, direction):
    density = state[0]
    momenta = state[1:4]
    energy = state[4]
    velocity = momenta / density
    pressure = GAMMA_LESS * (energy - 0.5 * jnp.sum(momenta * velocity, axis=0))
    moving = velocity[direction]
    pieces = [momenta[direction]]
    for component in range(3):
        term = momenta[component] * moving
        if component == direction:
            term = term + pressure
        pieces.append(term)
    pieces.append((energy + pressure) * moving)
    return jnp.stack(pieces)


def fluid_segment(flow_state):
    total_first = flow_state.shape[1]
    block_first = total_first // N_BRICK

    def one_block(brick_index):
        rows_taken = (brick_index * block_first + jnp.arange(-1, block_first + 1, dtype=jnp.int32)) % total_first
        slab = jnp.take(flow_state, rows_taken, axis=1)
        centre = slab[:, 1:-1]
        first_flux = flux_along(slab, 0)
        second_flux = flux_along(centre, 1)
        third_flux = flux_along(centre, 2)
        difference = (first_flux[:, 2:] - first_flux[:, :-2]) + (jnp.roll(second_flux, -1, 2) - jnp.roll(second_flux, 1, 2)) + (jnp.roll(third_flux, -1, 3) - jnp.roll(third_flux, 1, 3))
        smoothed = slab[:, 2:] + slab[:, :-2] + jnp.roll(centre, -1, 2) + jnp.roll(centre, 1, 2) + jnp.roll(centre, -1, 3) + jnp.roll(centre, 1, 3) - 6.0 * centre
        return centre - 0.5 * STEP_RATIO * difference + SMOOTHING * smoothed

    stacked = lax.map(one_block, jnp.arange(N_BRICK, dtype=jnp.int32))
    return jnp.moveaxis(stacked, 0, 1).reshape(flow_state.shape)


def shell_operator(vector_field, stiff_diag, stiff_chord, chord_before):
    padded = jnp.pad(vector_field, ((0, 0), (1, 1), (0, 0)))
    span_term = 2.0 * vector_field - padded[:, 2:] - padded[:, :-2]
    chord_term = stiff_chord * (vector_field - jnp.roll(vector_field, -1, 2)) + chord_before * (vector_field - jnp.roll(vector_field, 1, 2))
    return stiff_diag * vector_field + chord_term + span_term


def reference(flow_state, point_cell, normals, rbf_weights, block_owner, block_start, stiff_diag, stiff_chord):
    fluid_next = fluid_segment(flow_state)
    devices = N_BRICK * N_ROW
    pressure = pressure_of(flow_state)
    total_first = pressure.shape[0]
    total_second = pressure.shape[1]
    per_device = pressure.reshape(N_BRICK, total_first // N_BRICK, N_ROW, total_second // N_ROW, -1)
    per_device = per_device.transpose(0, 2, 1, 3, 4).reshape(devices, -1)
    cells = point_cell.reshape(devices, -1)
    sampled = jnp.take_along_axis(per_device, cells, axis=1).reshape(point_cell.shape)
    traction = (sampled[None] * normals).astype(jnp.bfloat16)
    blocks_dev = point_cell.shape[0] // devices
    traction_dev = traction.reshape(3, devices, blocks_dev, BP).transpose(1, 0, 2, 3)
    weights_dev = rbf_weights.reshape(devices, blocks_dev, BP, BW)

    def one_device(pair):
        return jnp.einsum("cbp,bpw->cbw", pair[0].astype(jnp.float32), pair[1].astype(jnp.float32))

    block_force = lax.map(one_device, (traction_dev, weights_dev))
    block_force = block_force.transpose(1, 0, 2, 3).reshape(3, -1, BW)
    span_nodes = SR_DEV * CHORD
    columns = (block_owner[:, 0] * span_nodes + block_start)[:, None] + jnp.arange(BW, dtype=jnp.int32)[None, :]
    loads = jnp.zeros((3, N_ROW * span_nodes), jnp.float32).at[:, columns.reshape(-1)].add(block_force.reshape(3, -1))
    loads = loads.reshape(3, SR_DEV * N_ROW, CHORD)
    chord_before = jnp.roll(stiff_chord, 1, 1)
    displacement = jnp.zeros_like(loads)
    residual = loads
    direction = loads
    norm_now = jnp.sum(residual * residual)
    for iteration in range(ITERS):
        image = shell_operator(direction, stiff_diag, stiff_chord, chord_before)
        step_length = norm_now / jnp.sum(direction * image)
        displacement = displacement + step_length * direction
        residual = residual - step_length * image
        norm_next = jnp.sum(residual * residual)
        direction = residual + (norm_next / norm_now) * direction
        norm_now = norm_next
    return fluid_next, displacement, residual
```

```python
import jax
import jax.numpy as jnp
from jax import lax
from jax.experimental import pallas as pl
from jax.experimental.pallas import tpu as pltpu
from jax.sharding import PartitionSpec as P

NX = 8
NY = 8
NBRICK = NX * NY
NROW = 16
NBLK = 16
BP = 64
SPAN = 8
HALO = 3
ROWS = SPAN + 2 * HALO
CENTRE = 4.0
WIDTH = 4.0
PRESSURE = 0.4
FLUX = 0.05
SMOOTH = 0.1
MESH = pl.DeviceIdType.MESH
F32 = jnp.float32
BF16 = jnp.bfloat16


def iota(shape, axis):
    return lax.broadcasted_iota(jnp.int32, shape, axis)


def three_terms(value):
    first = value.astype(BF16)
    rest = value - first.astype(F32)
    second = rest.astype(BF16)
    third = (rest - second.astype(F32)).astype(BF16)
    return first, second, third


def select_rows(chosen, values):
    chosen = chosen.astype(F32).astype(BF16)
    parts = [jnp.dot(chosen, term, preferred_element_type=F32) for term in three_terms(values)]
    return parts[0] + (parts[1] + parts[2])


def take_lanes(values, index):
    return jnp.take_along_axis(values, index, axis=1, mode="promise_in_bounds")


def sample_pressure(flow, cell, packed_cell, pressure):
    density = flow[0:32, :]
    inverse = 1.0 / density
    kinetic = jnp.zeros_like(density)
    for c in range(3):
        momentum = flow[32 * (c + 1) : 32 * (c + 2), :]
        kinetic = kinetic + momentum * (momentum * inverse)
    pressure[...] = PRESSURE * (flow[128:160, :] - 0.5 * kinetic)
    packed_cell[:, 0:BP] = cell[0:8, :]
    packed_cell[:, BP:128] = cell[8:16, :]
    index = packed_cell[...]
    high = index >> 7
    low = index & 127
    sampled = jnp.zeros((8, 128), F32)
    for k in range(32):
        line = jnp.broadcast_to(pressure[k : k + 1, :], (8, 128))
        sampled = jnp.where(high == k, take_lanes(line, low), sampled)
    return jnp.concatenate([sampled, pltpu.roll(sampled, BP, 1)], axis=0)[:, 0:BP]


def pack_windows(sampled, normals, weights, owner, start, send):
    traction = jnp.concatenate([(sampled * normals[c]).astype(BF16) for c in range(3)], axis=0)
    block_of_row = iota((48, 128), 0) & 15
    forces = jnp.zeros((48, 128), F32)
    for b in range(NBLK):
        product = jnp.dot(traction, weights[b], preferred_element_type=F32)
        forces = jnp.where(block_of_row == b, product, forces)
    block = (iota((16, 128), 1) & 15).astype(F32)
    named = jnp.broadcast_to(owner[...], (16, 128))
    begins = jnp.broadcast_to(start[...], (16, 128)).astype(F32)
    mine = named == iota((16, 128), 0)
    first = jnp.min(jnp.where(mine, block, 999.0), axis=1, keepdims=True)
    is_first = jnp.where(mine & (block == first), 1.0, 0.0)
    is_first = jnp.sum(is_first, axis=0, keepdims=True)
    key = 2.0 * named[0:1, :].astype(F32) + (1.0 - is_first)
    key = jnp.broadcast_to(key, (128, 128))
    row = iota((128, 128), 0)
    lane = iota((128, 128), 1)
    wanted = (2 * (row >> 3) + (row & 1)).astype(F32)
    match = key == wanted
    begin = jnp.sum(
        jnp.where(match, jnp.broadcast_to(begins[0:1, :], (128, 128)), 0.0), axis=1, keepdims=True
    )
    begin = jnp.broadcast_to(begin, (128, 128))
    chosen = match & ((lane >> 4) == ((row & 7) >> 1))
    windows = select_rows(chosen[:, 0:48], forces)
    shift = begin.astype(jnp.int32) & 127
    index = (lane - shift) & 127
    for o in range(NROW):
        part = slice(8 * o, 8 * o + 8)
        turned = take_lanes(windows[part], index[part])
        send[o] = jnp.where((row[part] & 7) < 6, turned, begin[part])


def add_windows(received, dense):
    values = received[...].reshape(128, 128)
    low = jnp.broadcast_to(received[:, 6:7, :], (16, 8, 128)).reshape(128, 128)
    high = jnp.broadcast_to(received[:, 7:8, :], (16, 8, 128)).reshape(128, 128)
    row = iota((128, 128), 0)
    lane = iota((128, 128), 1)
    begin = jnp.where((row & 1) == 0, low, high)
    shift = begin.astype(jnp.int32) & 127
    upright = jnp.sum(jnp.where(row == lane, begin, 0.0), axis=0, keepdims=True)
    line = jnp.broadcast_to(upright.astype(jnp.int32) >> 7, (128, 128))
    component = (lane & 7) >> 1
    fits = (component == ((row >> 2) & 3)) & (component < 3)
    place = 4 * (row >> 4) + (row & 3)
    window = (row & 7) < 6
    total = select_rows(fits & (place == line), jnp.where(window & (lane >= shift), values, 0.0))
    total = total + select_rows(fits & (place == line + 1), jnp.where(window & (lane < shift), values, 0.0))
    dense[...] = total.reshape(SPAN, 16, 128)


def turn(value, by, axis):
    size = value.shape[axis]
    return pltpu.roll(value, by % size, axis)


def next_node(value):
    turned = turn(value, -1, 1)
    sub = iota((8, 128), 0) & 3
    ahead = jnp.where(sub == 3, turn(turned, 3, 0), turn(turned, -1, 0))
    return jnp.where(iota((8, 128), 1) == 127, ahead, turned)


def node_before(value):
    turned = turn(value, 1, 1)
    sub = iota((8, 128), 0) & 3
    behind = jnp.where(sub == 0, turn(turned, -3, 0), turn(turned, 1, 0))
    return jnp.where(iota((8, 128), 1) == 0, behind, turned)


def pieces_along(state, direction):
    density, energy = state[0], state[4]
    inverse = 1.0 / density
    velocity = [state[1 + c] * inverse for c in range(3)]
    kinetic = state[1] * velocity[0] + state[2] * velocity[1] + state[3] * velocity[2]
    pressure = PRESSURE * (energy - 0.5 * kinetic)
    moving = velocity[direction]
    flux = [state[1 + direction]]
    for c in range(3):
        term = state[1 + c] * moving
        flux.append(term + pressure if c == direction else term)
    flux.append((energy + pressure) * moving)
    ahead = [SMOOTH * s + FLUX * f for s, f in zip(state, flux)]
    behind = [SMOOTH * s - FLUX * f for s, f in zip(state, flux)]
    return ahead, behind


def fluid_step(flow, x_low, x_high, y_low, y_high, result):
    own = [[flow[32 * f + 8 * i : 32 * f + 8 * i + 8, :] for f in range(5)] for i in range(4)]
    total = [[(1.0 - 6.0 * SMOOTH) * own[i][f] for f in range(5)] for i in range(4)]
    slab = [[x_low[f] for f in range(5)]] + own + [[x_high[f] for f in range(5)]]
    for i in range(6):
        ahead, behind = pieces_along(slab[i], 0)
        for f in range(5):
            if i <= 3:
                total[i][f] = total[i][f] + ahead[f]
            if i >= 2:
                total[i - 2][f] = total[i - 2][f] + behind[f]
    from_low, _ = pieces_along([y_low[4 * f : 4 * f + 4, :] for f in range(5)], 1)
    _, from_high = pieces_along([y_high[4 * f : 4 * f + 4, :] for f in range(5)], 1)
    sub = iota((8, 128), 0)
    for i in range(4):
        ahead, behind = pieces_along(own[i], 1)
        for f in range(5):
            low = jnp.broadcast_to(from_low[f][i : i + 1, :], (8, 128))
            high = jnp.broadcast_to(from_high[f][i : i + 1, :], (8, 128))
            total[i][f] = total[i][f] + jnp.where(sub == 0, low, turn(ahead[f], 1, 0))
            total[i][f] = total[i][f] + jnp.where(sub == 7, high, turn(behind[f], -1, 0))
        ahead, behind = pieces_along(own[i], 2)
        for f in range(5):
            total[i][f] = total[i][f] + turn(ahead[f], 1, 1) + turn(behind[f], -1, 1)
            result[32 * f + 8 * i : 32 * f + 8 * i + 8, :] = total[i][f]


def lay_stiffness(source, target):
    for s in range(SPAN):
        for j in range(4):
            line = source[s : s + 1, 128 * j : 128 * j + 128]
            target[s, j : j + 1, :] = line
            target[s, 4 + j : 5 + j, :] = line


def kernel(
    flow, cell, normals, weights, owner, start, stiff_diag, stiff_chord,
    fluid_next, displacement, residual,
    packed_cell, pressure, windows_out, windows_in, dense, x_in, x_sum, y_in, lines,
    shares_out, shares_in, y_edges, x_low, x_high, y_low, y_high,
    diag_rows, chord_rows, diag_halo, chord_halo, fields, turned,
    send_sem, recv_sem, fluid_send, fluid_recv, stiff_send, stiff_recv,
):
    brick = lax.axis_index("brick")
    row = lax.axis_index("row")
    x = lax.div(brick, NY)
    y = lax.rem(brick, NY)
    row_up = lax.rem(row + 1, NROW)
    row_down = lax.rem(row + NROW - 1, NROW)
    brick_up = lax.rem(brick + 1, NBRICK)
    brick_down = lax.rem(brick + NBRICK - 1, NBRICK)

    def x_peer(k):
        return lax.rem(x + k, NX) * NY + y

    def y_peer(k):
        return x * NY + lax.rem(y + k, NY)

    barrier = pltpu.get_barrier_semaphore()

    def greet(to_brick, to_row):
        pl.semaphore_signal(barrier, inc=1, device_id=(to_brick, to_row), device_id_type=MESH)

    @pl.loop(1, NROW)
    def _(k):
        greet(brick, lax.rem(row + k, NROW))

    @pl.loop(1, NX)
    def _(k):
        greet(x_peer(k), row)
        greet(x_peer(k), row_up)
        greet(x_peer(k), row_down)

    @pl.loop(1, NY)
    def _(k):
        greet(y_peer(k), row)

    greet(brick_up, row)
    greet(brick_down, row)

    def copy_to(source, target, send, receive, to_brick, to_row):
        return pltpu.make_async_remote_copy(
            src_ref=source, dst_ref=target, send_sem=send, recv_sem=receive,
            device_id=(to_brick, to_row), device_id_type=MESH,
        )

    sampled = sample_pressure(flow, cell, packed_cell, pressure)
    pack_windows(sampled, normals, weights, owner, start, windows_out)
    y_edges[...] = jnp.zeros((2, 24, 128), F32)
    y_edges[0, 0:20, :] = flow[pl.ds(0, 20, stride=8), :]
    y_edges[1, 0:20, :] = flow[pl.ds(7, 20, stride=8), :]

    pl.semaphore_wait(barrier, (NROW - 1) + 3 * (NX - 1) + (NY - 1) + 2)

    @pl.loop(1, NROW)
    def _(k):
        to = lax.rem(row + k, NROW)
        copy_to(windows_out.at[to], windows_in.at[row], send_sem.at[0], recv_sem.at[0], brick, to).start()

    windows_in[row] = windows_out[row]

    fluid_copies = [
        copy_to(y_edges.at[0], y_high, fluid_send.at[0], fluid_recv.at[0], brick, row_down),
        copy_to(y_edges.at[1], y_low, fluid_send.at[1], fluid_recv.at[1], brick, row_up),
    ]
    for f in range(5):
        plane = flow.at[pl.ds(32 * f, 8)]
        fluid_copies.append(
            copy_to(plane, x_high.at[f], fluid_send.at[2 + f], fluid_recv.at[2 + f], brick_down, row)
        )
        plane = flow.at[pl.ds(32 * f + 24, 8)]
        fluid_copies.append(
            copy_to(plane, x_low.at[f], fluid_send.at[7 + f], fluid_recv.at[7 + f], brick_up, row)
        )
    for copy in fluid_copies:
        copy.start()
    lay_stiffness(stiff_diag, diag_rows)
    lay_stiffness(stiff_chord, chord_rows)
    stiff_copies = []
    for n, (rows, halo) in enumerate(((diag_rows, diag_halo), (chord_rows, chord_halo))):
        stiff_copies.append(
            copy_to(rows.at[pl.ds(SPAN - 2, 2)], halo.at[0], stiff_send.at[2 * n], stiff_recv.at[2 * n], brick, row_up)
        )
        stiff_copies.append(
            copy_to(rows.at[pl.ds(0, 2)], halo.at[1], stiff_send.at[2 * n + 1], stiff_recv.at[2 * n + 1], brick, row_down)
        )
    for copy in stiff_copies:
        copy.start()

    def await_copies(buffer, count, n):
        part = buffer.at[pl.ds(0, count)]
        copy_to(part, part, send_sem.at[n], recv_sem.at[n], brick_up, row).wait_recv()

    await_copies(windows_in, NROW - 1, 0)
    add_windows(windows_in, dense)

    @pl.loop(1, NX)
    def _(k):
        to = lax.rem(x + k, NX)
        copy_to(dense.at[to], x_in.at[x], send_sem.at[1], recv_sem.at[1], x_peer(k), row).start()

    x_in[x] = dense[x]
    await_copies(x_in, NX - 1, 1)
    total = x_in[0]
    for k in range(1, NX):
        total = total + x_in[k]
    x_sum[...] = total

    @pl.loop(1, NY)
    def _(k):
        copy_to(x_sum, y_in.at[y], send_sem.at[2], recv_sem.at[2], y_peer(k), row).start()

    y_in[y] = total

    for copy in fluid_copies:
        copy.wait_recv()
    fluid_step(flow, x_low, x_high, y_low, y_high, fluid_next)
    for copy in stiff_copies:
        copy.wait_recv()

    await_copies(y_in, NY - 1, 2)
    total = y_in[0]
    for k in range(1, NY):
        total = total + y_in[k]
    lines[HALO + x] = total

    own_line = lines.at[HALO + x]

    @pl.loop(1, NX)
    def _(k):
        copy_to(own_line, own_line, send_sem.at[3], recv_sem.at[3], x_peer(k), row).start()

    goes_up = (x >= SPAN - HALO) & (row < NROW - 1)
    goes_down = (x < HALO) & (row > 0)

    @pl.when(goes_up)
    def _():
        @pl.loop(0, NX)
        def _(k):
            copy_to(own_line, lines.at[x - (SPAN - HALO)], send_sem.at[4], recv_sem.at[4], x_peer(k), row_up).start()

    @pl.when(goes_down)
    def _():
        @pl.loop(0, NX)
        def _(k):
            target = lines.at[HALO + SPAN + x]
            copy_to(own_line, target, send_sem.at[5], recv_sem.at[5], x_peer(k), row_down).start()

    @pl.when(row == 0)
    def _():
        lines[0:HALO] = jnp.zeros((HALO, 16, 128), F32)

    @pl.when(row == NROW - 1)
    def _():
        lines[HALO + SPAN : ROWS] = jnp.zeros((HALO, 16, 128), F32)

    await_copies(lines, NX - 1, 3)

    @pl.when(row > 0)
    def _():
        await_copies(lines, HALO, 4)

    @pl.when(row < NROW - 1)
    def _():
        await_copies(lines, HALO, 5)

    below = jnp.where(row > 0, 1.0, 0.0).astype(F32)
    above = jnp.where(row < NROW - 1, 1.0, 0.0).astype(F32)
    diag = [None, diag_halo[0, 0], diag_halo[0, 1]] + [diag_rows[s] for s in range(SPAN)]
    diag = diag + [diag_halo[1, 0], diag_halo[1, 1]]
    chord = [None, chord_halo[0, 0], chord_halo[0, 1]] + [chord_rows[s] for s in range(SPAN)]
    chord = chord + [chord_halo[1, 0], chord_halo[1, 1]]
    diag = [None if d is None else (d + (2.0 - CENTRE)) * (1.0 / WIDTH) for d in diag]
    chord = [None if d is None else d * (1.0 / WIDTH) for d in chord]
    products = [jnp.zeros((8, 128), F32) for _ in range(6)]
    for half in range(2):
        part = slice(8 * half, 8 * half + 8)
        levels = [[lines[i, part, :] for i in range(ROWS)]]
        for level in range(1, HALO + 1):
            before = levels[-1]
            after = [None] * ROWS
            for i in range(level, ROWS - level):
                flow_on = chord[i] * (before[i] - next_node(before[i]))
                value = diag[i] * before[i] + (flow_on - node_before(flow_on))
                value = value - (1.0 / WIDTH) * (before[i - 1] + before[i + 1])
                if i < HALO:
                    value = value * below
                if i >= HALO + SPAN:
                    value = value * above
                after[i] = value
            levels.append(after)
        for i in range(HALO, HALO + SPAN):
            for level in range(HALO + 1):
                fields[level, i - HALO, part, :] = levels[level][i]
            for n, (p, q) in enumerate(((0, 0), (0, 1), (1, 1), (1, 2), (2, 2), (2, 3))):
                products[n] = products[n] + levels[p][i] * levels[q][i]
    shares_out[...] = jnp.zeros((8, 128), F32)
    for n in range(6):
        shares_out[n : n + 1, :] = jnp.sum(products[n], axis=0, keepdims=True)

    @pl.loop(1, NROW)
    def _(k):
        to = lax.rem(row + k, NROW)
        copy_to(shares_out, shares_in.at[row], send_sem.at[6], recv_sem.at[6], brick, to).start()

    shares_in[row] = shares_out[...]

    for level in range(HALO + 1):
        for s in range(SPAN):
            for c in range(3):
                for j in range(4):
                    line = fields[level, s, 4 * c + j : 4 * c + j + 1, :]
                    turned[level, c, s : s + 1, 128 * j : 128 * j + 128] = line

    await_copies(shares_in, NROW - 1, 6)
    share = shares_in[0]
    for k in range(1, NROW):
        share = share + shares_in[k]
    share = jnp.broadcast_to(jnp.sum(share, axis=1, keepdims=True), (8, 128))
    moment = [jnp.broadcast_to(share[n : n + 1, :], (8, 128)) for n in range(6)]
    matrix = [CENTRE * moment[n] + WIDTH * moment[n + 1] for n in range(5)]
    m00, m01, m02, m11, m12, m22 = matrix[0], matrix[1], matrix[2], matrix[2], matrix[3], matrix[4]
    l10 = m01 / m00
    l20 = m02 / m00
    d1 = m11 - l10 * m01
    e = m12 - l10 * m02
    l21 = e / d1
    d2 = m22 - l20 * m02 - l21 * e
    y1 = moment[1] - l10 * moment[0]
    y2 = moment[2] - l20 * moment[0] - l21 * y1
    w2 = y2 / d2
    w1 = y1 / d1 - l21 * w2
    w0 = moment[0] / m00 - l10 * w1 - l20 * w2
    r0 = 1.0 - CENTRE * w0
    r1 = -(WIDTH * w0 + CENTRE * w1)
    r2 = -(WIDTH * w1 + CENTRE * w2)
    r3 = -(WIDTH * w2)
    for c in range(3):
        for j in range(4):
            part = slice(128 * j, 128 * j + 128)
            v = [turned[level, c, :, part] for level in range(4)]
            displacement[c, :, part] = w0 * v[0] + w1 * v[1] + w2 * v[2]
            residual[c, :, part] = (r0 * v[0] + r1 * v[1]) + (r2 * v[2] + r3 * v[3])

    def await_sent(buffer, count, n):
        part = buffer.at[pl.ds(0, count)]
        copy_to(part, part, send_sem.at[n], recv_sem.at[n], brick_up, row).wait_send()

    await_sent(windows_in, NROW - 1, 0)
    await_sent(x_in, NX - 1, 1)
    await_sent(y_in, NY - 1, 2)
    await_sent(lines, NX - 1, 3)

    @pl.when(goes_up)
    def _():
        await_sent(lines, NX, 4)

    @pl.when(goes_down)
    def _():
        await_sent(lines, NX, 5)

    await_sent(shares_in, NROW - 1, 6)
    for copy in fluid_copies + stiff_copies:
        copy.wait_send()


def per_device(
    flow_state, point_cell, normals, rbf_weights, block_owner, block_start, stiff_diag, stiff_chord
):
    flow = flow_state.reshape(160, 128)
    owner = jnp.tile(block_owner.reshape(1, NBLK), (1, 3))
    owner = jnp.pad(owner, ((0, 0), (0, 128 - 3 * NBLK)), constant_values=-1)
    start = jnp.pad(block_start.reshape(1, NBLK), ((0, 0), (0, 128 - NBLK)))
    vmem = pl.BlockSpec(memory_space=pltpu.VMEM)
    dma = pltpu.SemaphoreType.DMA
    fluid_next, displacement, residual = pl.pallas_call(
        kernel,
        out_shape=(
            jax.ShapeDtypeStruct((160, 128), F32),
            jax.ShapeDtypeStruct((3, SPAN, 512), F32),
            jax.ShapeDtypeStruct((3, SPAN, 512), F32),
        ),
        in_specs=[vmem] * 8,
        out_specs=(vmem, vmem, vmem),
        scratch_shapes=[
            pltpu.VMEM((8, 128), jnp.int32),
            pltpu.VMEM((32, 128), F32),
            pltpu.VMEM((NROW, 8, 128), F32),
            pltpu.VMEM((NROW, 8, 128), F32),
            pltpu.VMEM((SPAN, 16, 128), F32),
            pltpu.VMEM((NX, 16, 128), F32),
            pltpu.VMEM((16, 128), F32),
            pltpu.VMEM((NY, 16, 128), F32),
            pltpu.VMEM((ROWS, 16, 128), F32),
            pltpu.VMEM((8, 128), F32),
            pltpu.VMEM((NROW, 8, 128), F32),
            pltpu.VMEM((2, 24, 128), F32),
            pltpu.VMEM((5, 8, 128), F32),
            pltpu.VMEM((5, 8, 128), F32),
            pltpu.VMEM((24, 128), F32),
            pltpu.VMEM((24, 128), F32),
            pltpu.VMEM((SPAN, 8, 128), F32),
            pltpu.VMEM((SPAN, 8, 128), F32),
            pltpu.VMEM((2, 2, 8, 128), F32),
            pltpu.VMEM((2, 2, 8, 128), F32),
            pltpu.VMEM((HALO + 1, SPAN, 16, 128), F32),
            pltpu.VMEM((HALO + 1, 3, SPAN, 512), F32),
            dma((7,)),
            dma((7,)),
            dma((12,)),
            dma((12,)),
            dma((4,)),
            dma((4,)),
        ],
        compiler_params=pltpu.CompilerParams(
            collective_id=0, has_side_effects=True, vmem_limit_bytes=16 * 1024 * 1024
        ),
        cost_estimate=pl.CostEstimate(flops=20_000_000, bytes_accessed=600_000, transcendentals=0),
        name="coupling_step",
    )(flow, point_cell, normals, rbf_weights, owner, start, stiff_diag, stiff_chord)
    return fluid_next.reshape(5, 4, 8, 128), displacement, residual


def solution(mesh):
    return jax.shard_map(
        per_device,
        mesh=mesh,
        in_specs=(
            P(None, "brick", "row", None),
            P(("brick", "row"), None),
            P(None, ("brick", "row"), None),
            P(("brick", "row"), None, None),
            P(("brick", "row"), None),
            P(("brick", "row")),
            P("row", None),
            P("row", None),
        ),
        out_specs=(P(None, "brick", "row", None), P(None, "row", None), P(None, "row", None)),
        check_vma=False,
    )
```

```python
import jax
import jax.numpy as jnp
from jax import lax
from jax.experimental import pallas as pl
from jax.experimental.pallas import tpu as pltpu
from jax.sharding import PartitionSpec as P

NX = 8
NY = 8
NBRICK = NX * NY
NROW = 16
NBLK = 16
BP = 64
SPAN = 8
HALO = 3
ROWS = SPAN + 2 * HALO
LINE = 12
FAR_FIRST = (4, 3, 5, 2, 6, 1, 7)
ROW_FAR_FIRST = (8, 7, 9, 6, 10, 5, 11, 4, 12, 3, 13, 2, 14, 1, 15)
CENTRE = 4.0
WIDTH = 4.0
PRESSURE = 0.4
FLUX = 0.05
SMOOTH = 0.1
MESH = pl.DeviceIdType.MESH
F32 = jnp.float32
BF16 = jnp.bfloat16


def iota(shape, axis):
    return lax.broadcasted_iota(jnp.int32, shape, axis)


def select_rows(chosen, values):
    first = values.astype(BF16)
    second = (values - first.astype(F32)).astype(BF16)
    terms = jnp.concatenate([first, second], axis=1)
    both = jnp.dot(chosen.astype(F32).astype(BF16), terms, preferred_element_type=F32)
    return both[:, 0:128] + both[:, 128:256]


def take_lanes(values, index):
    return jnp.take_along_axis(values, index, axis=1, mode="promise_in_bounds")


def sample_pressure(flow, cell, packed_cell, pressure):
    density = flow[0:32, :]
    inverse = 1.0 / density
    kinetic = jnp.zeros_like(density)
    for c in range(3):
        momentum = flow[32 * (c + 1) : 32 * (c + 2), :]
        kinetic = kinetic + momentum * (momentum * inverse)
    pressure[...] = PRESSURE * (flow[128:160, :] - 0.5 * kinetic)
    packed_cell[:, 0:BP] = cell[0:8, :]
    packed_cell[:, BP:128] = cell[8:16, :]
    index = packed_cell[...]
    high = index >> 7
    low = index & 127
    sampled = jnp.zeros((8, 128), F32)
    for k in range(32):
        line = jnp.broadcast_to(pressure[k : k + 1, :], (8, 128))
        sampled = jnp.where(high == k, take_lanes(line, low), sampled)
    swapped = pltpu.roll(sampled, BP, 1)
    left = iota((8, 128), 1) < BP
    return jnp.concatenate(
        [jnp.where(left, sampled, swapped), jnp.where(left, swapped, sampled)], axis=0
    )


def sort_blocks(owner, start, line_of):
    line_of[0:1, :] = jnp.full((1, 128), -1, jnp.int32)
    line_of[1:2, :] = jnp.zeros((1, 128), jnp.int32)
    line_of[0:1, 0:NBLK] = owner[...]
    line_of[1:2, 0:NBLK] = start[...]
    lane = iota((16, 128), 1).astype(F32)
    named = jnp.broadcast_to(line_of[0:1, :], (16, 128))
    mine = named == iota((16, 128), 0)
    first = jnp.min(jnp.where(mine, lane, 999.0), axis=1, keepdims=True)
    is_first = jnp.sum(jnp.where(mine & (lane == first), 1.0, 0.0), axis=0, keepdims=True)
    key = 2.0 * named[0:1, :].astype(F32) + (1.0 - is_first)
    key = jnp.broadcast_to(key, (128, 128))
    begins = jnp.broadcast_to(line_of[1:2, :].astype(F32), (128, 128))
    row = iota((128, 128), 0)
    wanted = (2 * (row >> 3) + (row & 1)).astype(F32)
    begin = jnp.sum(jnp.where(key == wanted, begins, 0.0), axis=1, keepdims=True)
    key = jnp.where(iota((128, 128), 1) < NBLK, key, -1.0)
    again = jnp.maximum(key, jnp.maximum(shifted(key, 16), shifted(key, 32)))
    component = iota((128, 128), 1) >> 4
    chosen = (again == wanted) & (component == ((row & 7) >> 1))
    return chosen[:, 0:48], jnp.broadcast_to(begin, (128, 128))


def shifted(value, by):
    return jnp.broadcast_to(pltpu.roll(value[0:8], by, 1)[0:1], value.shape)


def pack_windows(sampled, normals, doubled, weights, chosen, begin, send):
    doubled[:, :, 0:BP] = normals[...]
    doubled[:, :, BP:128] = normals[...]
    traction = jnp.concatenate([sampled * doubled[c] for c in range(3)], axis=0)
    block = iota((48, 128), 0) & 15
    half = iota((48, 128), 1) >> 6
    spread = [jnp.where(block == 2 * g + half, traction, 0.0).astype(BF16) for g in range(8)]
    forces = jnp.dot(jnp.concatenate(spread, axis=1), weights[...], preferred_element_type=F32)
    windows = select_rows(chosen, forces)
    index = (iota((128, 128), 1) - (begin.astype(jnp.int32) & 127)) & 127
    sub = iota((8, 128), 0)
    for o in range(NROW):
        part = slice(8 * o, 8 * o + 8)
        turned = take_lanes(windows[part], index[part])
        send[o] = jnp.where(sub < 6, turned, begin[part])


def add_windows(received, dense):
    values = received[...].reshape(128, 128)
    low = jnp.broadcast_to(received[:, 6:7, :], (16, 8, 128)).reshape(128, 128)
    high = jnp.broadcast_to(received[:, 7:8, :], (16, 8, 128)).reshape(128, 128)
    row = iota((128, 128), 0)
    lane = iota((128, 128), 1)
    begin = jnp.where((row & 1) == 0, low, high)
    shift = begin.astype(jnp.int32) & 127
    upright = jnp.sum(jnp.where(row == lane, begin, 0.0), axis=0, keepdims=True)
    line = jnp.broadcast_to(upright.astype(jnp.int32) >> 7, (128, 128))
    component = (lane & 7) >> 1
    fits = (component == ((row >> 2) & 3)) & (component < 3)
    place = 4 * (row >> 4) + (row & 3)
    window = (row & 7) < 6
    here = jnp.where(window & (lane >= shift), values, 0.0)
    after = jnp.where(window & (lane < shift), values, 0.0)
    chosen = jnp.concatenate([fits & (place == line), fits & (place == line + 1)], axis=1)
    total = select_rows(chosen, jnp.concatenate([here, after], axis=0))
    for s in range(SPAN):
        dense[s] = total[16 * s : 16 * s + LINE]


def turn(value, by, axis):
    size = value.shape[axis]
    return pltpu.roll(value, by % size, axis)


def next_node(value):
    turned = turn(value, -1, 1)
    sub = iota((8, 128), 0) & 3
    ahead = jnp.where(sub == 3, turn(turned, 3, 0), turn(turned, -1, 0))
    return jnp.where(iota((8, 128), 1) == 127, ahead, turned)


def node_before(value):
    turned = turn(value, 1, 1)
    sub = iota((8, 128), 0) & 3
    behind = jnp.where(sub == 0, turn(turned, -3, 0), turn(turned, 1, 0))
    return jnp.where(iota((8, 128), 1) == 0, behind, turned)


def pieces_along(state, direction):
    density, energy = state[0], state[4]
    inverse = 1.0 / density
    velocity = [state[1 + c] * inverse for c in range(3)]
    kinetic = state[1] * velocity[0] + state[2] * velocity[1] + state[3] * velocity[2]
    pressure = PRESSURE * (energy - 0.5 * kinetic)
    moving = velocity[direction]
    flux = [state[1 + direction]]
    for c in range(3):
        term = state[1 + c] * moving
        flux.append(term + pressure if c == direction else term)
    flux.append((energy + pressure) * moving)
    ahead = [SMOOTH * s + FLUX * f for s, f in zip(state, flux)]
    behind = [SMOOTH * s - FLUX * f for s, f in zip(state, flux)]
    return ahead, behind


def fluid_step(flow, x_low, x_high, y_low, y_high, result):
    own = [[flow[32 * f + 8 * i : 32 * f + 8 * i + 8, :] for f in range(5)] for i in range(4)]
    total = [[(1.0 - 6.0 * SMOOTH) * own[i][f] for f in range(5)] for i in range(4)]
    slab = [[x_low[f] for f in range(5)]] + own + [[x_high[f] for f in range(5)]]
    for i in range(6):
        ahead, behind = pieces_along(slab[i], 0)
        for f in range(5):
            if i <= 3:
                total[i][f] = total[i][f] + ahead[f]
            if i >= 2:
                total[i - 2][f] = total[i - 2][f] + behind[f]
    from_low, _ = pieces_along([y_low[4 * f : 4 * f + 4, :] for f in range(5)], 1)
    _, from_high = pieces_along([y_high[4 * f : 4 * f + 4, :] for f in range(5)], 1)
    sub = iota((8, 128), 0)
    for i in range(4):
        ahead, behind = pieces_along(own[i], 1)
        for f in range(5):
            low = jnp.broadcast_to(from_low[f][i : i + 1, :], (8, 128))
            high = jnp.broadcast_to(from_high[f][i : i + 1, :], (8, 128))
            total[i][f] = total[i][f] + jnp.where(sub == 0, low, turn(ahead[f], 1, 0))
            total[i][f] = total[i][f] + jnp.where(sub == 7, high, turn(behind[f], -1, 0))
        ahead, behind = pieces_along(own[i], 2)
        for f in range(5):
            total[i][f] = total[i][f] + turn(ahead[f], 1, 1) + turn(behind[f], -1, 1)
            result[32 * f + 8 * i : 32 * f + 8 * i + 8, :] = total[i][f]


def lay_stiffness(source, target):
    for s in range(SPAN):
        for j in range(4):
            line = source[s : s + 1, 128 * j : 128 * j + 128]
            target[s, j : j + 1, :] = line
            target[s, 4 + j : 5 + j, :] = line


def kernel(
    flow_far, cell_far, normals_far, weights_far, owner_far, start_far, diag_far, chord_far,
    fluid_next, displacement, residual,
    flow, cell, normals, weights, owner, start, stiff_diag, stiff_chord,
    packed_cell, line_of, doubled, pressure, windows_out, windows_in, dense, x_in, x_sum, y_in, lines,
    shares_out, shares_in, y_edges, x_low, x_high, y_low, y_high,
    diag_rows, chord_rows, diag_halo, chord_halo, fields, turned,
    load_sem, send_sem, recv_sem, fluid_send, fluid_recv, stiff_send, stiff_recv,
):
    brick = lax.axis_index("brick")
    row = lax.axis_index("row")
    x = lax.div(brick, NY)
    y = lax.rem(brick, NY)
    row_up = lax.rem(row + 1, NROW)
    row_down = lax.rem(row + NROW - 1, NROW)
    brick_up = lax.rem(brick + 1, NBRICK)
    brick_down = lax.rem(brick + NBRICK - 1, NBRICK)

    def x_peer(k):
        return lax.rem(x + k, NX) * NY + y

    def y_peer(k):
        return x * NY + lax.rem(y + k, NY)

    barrier = pltpu.get_barrier_semaphore()

    def greet(to_brick, to_row):
        pl.semaphore_signal(barrier, inc=1, device_id=(to_brick, to_row), device_id_type=MESH)

    for k in ROW_FAR_FIRST:
        greet(brick, lax.rem(row + k, NROW))

    loads = [
        pltpu.make_async_copy(far, near, load_sem.at[n])
        for n, (far, near) in enumerate((
            (flow_far, flow), (cell_far, cell), (weights_far, weights), (normals_far, normals),
            (owner_far, owner), (start_far, start), (diag_far, stiff_diag), (chord_far, stiff_chord),
        ))
    ]
    for load in loads:
        load.start()

    for k in FAR_FIRST:
        greet(x_peer(k), row)
        greet(y_peer(k), row)
    for k in FAR_FIRST:
        greet(x_peer(k), row_up)
        greet(x_peer(k), row_down)
    greet(brick_up, row)
    greet(brick_down, row)

    def copy_to(source, target, send, receive, to_brick, to_row):
        return pltpu.make_async_remote_copy(
            src_ref=source, dst_ref=target, send_sem=send, recv_sem=receive,
            device_id=(to_brick, to_row), device_id_type=MESH,
        )

    loads[4].wait()
    loads[5].wait()
    chosen, begin = sort_blocks(owner, start, line_of)
    loads[0].wait()
    loads[1].wait()
    sampled = sample_pressure(flow, cell, packed_cell, pressure)
    loads[2].wait()
    loads[3].wait()
    pack_windows(sampled, normals, doubled, weights, chosen, begin, windows_out)
    y_edges[...] = jnp.zeros((2, 24, 128), F32)
    y_edges[0, 0:20, :] = flow[pl.ds(0, 20, stride=8), :]
    y_edges[1, 0:20, :] = flow[pl.ds(7, 20, stride=8), :]

    pl.semaphore_wait(barrier, (NROW - 1) + 3 * (NX - 1) + (NY - 1) + 2)

    for k in ROW_FAR_FIRST:
        to = lax.rem(row + k, NROW)
        copy_to(windows_out.at[to], windows_in.at[row], send_sem.at[0], recv_sem.at[0], brick, to).start()

    windows_in[row] = windows_out[row]

    fluid_copies = [
        copy_to(y_edges.at[0], y_high, fluid_send.at[0], fluid_recv.at[0], brick, row_down),
        copy_to(y_edges.at[1], y_low, fluid_send.at[1], fluid_recv.at[1], brick, row_up),
    ]
    for f in range(5):
        plane = flow.at[pl.ds(32 * f, 8)]
        fluid_copies.append(
            copy_to(plane, x_high.at[f], fluid_send.at[2 + f], fluid_recv.at[2 + f], brick_down, row)
        )
        plane = flow.at[pl.ds(32 * f + 24, 8)]
        fluid_copies.append(
            copy_to(plane, x_low.at[f], fluid_send.at[7 + f], fluid_recv.at[7 + f], brick_up, row)
        )
    for copy in fluid_copies:
        copy.start()
    loads[6].wait()
    loads[7].wait()
    lay_stiffness(stiff_diag, diag_rows)
    lay_stiffness(stiff_chord, chord_rows)
    stiff_copies = []
    for n, (rows, halo) in enumerate(((diag_rows, diag_halo), (chord_rows, chord_halo))):
        stiff_copies.append(
            copy_to(rows.at[pl.ds(SPAN - 2, 2)], halo.at[0], stiff_send.at[2 * n], stiff_recv.at[2 * n], brick, row_up)
        )
        stiff_copies.append(
            copy_to(rows.at[pl.ds(0, 2)], halo.at[1], stiff_send.at[2 * n + 1], stiff_recv.at[2 * n + 1], brick, row_down)
        )
    for copy in stiff_copies:
        copy.start()

    def await_copies(buffer, count, n):
        part = buffer.at[pl.ds(0, count)]
        copy_to(part, part, send_sem.at[n], recv_sem.at[n], brick_up, row).wait_recv()

    await_copies(windows_in, NROW - 1, 0)
    add_windows(windows_in, dense)

    for k in FAR_FIRST:
        to = lax.rem(x + k, NX)
        copy_to(dense.at[to], x_in.at[x], send_sem.at[1], recv_sem.at[1], x_peer(k), row).start()

    x_in[x] = dense[x]
    await_copies(x_in, NX - 1, 1)
    total = x_in[0]
    for k in range(1, NX):
        total = total + x_in[k]
    x_sum[...] = total

    for k in FAR_FIRST:
        copy_to(x_sum, y_in.at[y], send_sem.at[2], recv_sem.at[2], y_peer(k), row).start()

    y_in[y] = total

    for copy in fluid_copies:
        copy.wait_recv()
    fluid_step(flow, x_low, x_high, y_low, y_high, fluid_next)
    for copy in stiff_copies:
        copy.wait_recv()

    await_copies(y_in, NY - 1, 2)
    total = y_in[0]
    for k in range(1, NY):
        total = total + y_in[k]
    lines[HALO + x] = total

    own_line = lines.at[HALO + x]

    goes_up = (x >= SPAN - HALO) & (row < NROW - 1)
    goes_down = (x < HALO) & (row > 0)

    def send_beside(steps):
        @pl.when(goes_up)
        def _():
            for k in steps:
                target = lines.at[x - (SPAN - HALO)]
                copy_to(own_line, target, send_sem.at[4], recv_sem.at[4], x_peer(k), row_up).start()

        @pl.when(goes_down)
        def _():
            for k in steps:
                target = lines.at[HALO + SPAN + x]
                copy_to(own_line, target, send_sem.at[5], recv_sem.at[5], x_peer(k), row_down).start()

    send_beside((4, 3, 5))
    for k in FAR_FIRST:
        copy_to(own_line, own_line, send_sem.at[3], recv_sem.at[3], x_peer(k), row).start()
    send_beside((2, 6, 1, 7, 0))

    @pl.when(row == 0)
    def _():
        lines[0:HALO] = jnp.zeros((HALO, LINE, 128), F32)

    @pl.when(row == NROW - 1)
    def _():
        lines[HALO + SPAN : ROWS] = jnp.zeros((HALO, LINE, 128), F32)

    await_copies(lines, NX - 1, 3)

    @pl.when(row > 0)
    def _():
        await_copies(lines, HALO, 4)

    @pl.when(row < NROW - 1)
    def _():
        await_copies(lines, HALO, 5)

    below = jnp.where(row > 0, 1.0, 0.0).astype(F32)
    above = jnp.where(row < NROW - 1, 1.0, 0.0).astype(F32)
    diag = [None, diag_halo[0, 0], diag_halo[0, 1]] + [diag_rows[s] for s in range(SPAN)]
    diag = diag + [diag_halo[1, 0], diag_halo[1, 1]]
    chord = [None, chord_halo[0, 0], chord_halo[0, 1]] + [chord_rows[s] for s in range(SPAN)]
    chord = chord + [chord_halo[1, 0], chord_halo[1, 1]]
    diag = [None if d is None else (d + (2.0 - CENTRE)) * (1.0 / WIDTH) for d in diag]
    chord = [None if d is None else d * (1.0 / WIDTH) for d in chord]
    products = [jnp.zeros((8, 128), F32) for _ in range(6)]
    for half in range(2):
        part = slice(8 * half, 8 * half + 8)
        if half == 0:
            levels = [[lines[i, 0:8, :] for i in range(ROWS)]]
        else:
            spare = jnp.zeros((4, 128), F32)
            levels = [[jnp.concatenate([lines[i, 8:LINE, :], spare], axis=0) for i in range(ROWS)]]
        for level in range(1, HALO + 1):
            before = levels[-1]
            after = [None] * ROWS
            for i in range(level, ROWS - level):
                flow_on = chord[i] * (before[i] - next_node(before[i]))
                value = diag[i] * before[i] + (flow_on - node_before(flow_on))
                value = value - (1.0 / WIDTH) * (before[i - 1] + before[i + 1])
                if i < HALO:
                    value = value * below
                if i >= HALO + SPAN:
                    value = value * above
                after[i] = value
            levels.append(after)
        for i in range(HALO, HALO + SPAN):
            for level in range(HALO + 1):
                fields[level, i - HALO, part, :] = levels[level][i]
            for n, (p, q) in enumerate(((0, 0), (0, 1), (1, 1), (1, 2), (2, 2), (2, 3))):
                products[n] = products[n] + levels[p][i] * levels[q][i]
    share = jnp.zeros((1, 128), F32)
    lane = iota((1, 128), 1)
    for n in range(6):
        inner = jnp.sum(jnp.sum(products[n], axis=0, keepdims=True), axis=1, keepdims=True)
        share = jnp.where(lane == n, jnp.broadcast_to(inner, (1, 128)), share)
    shares_out[...] = share

    for k in ROW_FAR_FIRST:
        to = lax.rem(row + k, NROW)
        copy_to(shares_out, shares_in.at[row], send_sem.at[6], recv_sem.at[6], brick, to).start()

    shares_in[row] = shares_out[...]

    for level in range(HALO + 1):
        for s in range(SPAN):
            for c in range(3):
                for j in range(4):
                    line = fields[level, s, 4 * c + j : 4 * c + j + 1, :]
                    turned[level, c, s : s + 1, 128 * j : 128 * j + 128] = line

    await_copies(shares_in, NROW - 1, 6)
    share = shares_in[0]
    for k in range(1, NROW):
        share = share + shares_in[k]
    moment = [jnp.broadcast_to(share[:, n : n + 1], (8, 128)) for n in range(6)]
    matrix = [CENTRE * moment[n] + WIDTH * moment[n + 1] for n in range(5)]
    m00, m01, m02, m11, m12, m22 = matrix[0], matrix[1], matrix[2], matrix[2], matrix[3], matrix[4]
    l10 = m01 / m00
    l20 = m02 / m00
    d1 = m11 - l10 * m01
    e = m12 - l10 * m02
    l21 = e / d1
    d2 = m22 - l20 * m02 - l21 * e
    y1 = moment[1] - l10 * moment[0]
    y2 = moment[2] - l20 * moment[0] - l21 * y1
    w2 = y2 / d2
    w1 = y1 / d1 - l21 * w2
    w0 = moment[0] / m00 - l10 * w1 - l20 * w2
    r0 = 1.0 - CENTRE * w0
    r1 = -(WIDTH * w0 + CENTRE * w1)
    r2 = -(WIDTH * w1 + CENTRE * w2)
    r3 = -(WIDTH * w2)
    for c in range(3):
        for j in range(4):
            part = slice(128 * j, 128 * j + 128)
            v = [turned[level, c, :, part] for level in range(4)]
            displacement[c, :, part] = w0 * v[0] + w1 * v[1] + w2 * v[2]
            residual[c, :, part] = (r0 * v[0] + r1 * v[1]) + (r2 * v[2] + r3 * v[3])

    def await_sent(buffer, count, n):
        part = buffer.at[pl.ds(0, count)]
        copy_to(part, part, send_sem.at[n], recv_sem.at[n], brick_up, row).wait_send()

    await_sent(windows_in, NROW - 1, 0)
    await_sent(x_in, NX - 1, 1)
    await_sent(y_in, NY - 1, 2)
    await_sent(lines, NX - 1, 3)

    @pl.when(goes_up)
    def _():
        await_sent(lines, NX, 4)

    @pl.when(goes_down)
    def _():
        await_sent(lines, NX, 5)

    await_sent(shares_in, NROW - 1, 6)
    for copy in fluid_copies + stiff_copies:
        copy.wait_send()


def write_out(fluid, displacement, residual, fluid_far, displacement_far, residual_far, sem):
    copies = [
        pltpu.make_async_copy(near, far, sem.at[n])
        for n, (near, far) in enumerate(
            ((fluid, fluid_far), (displacement, displacement_far), (residual, residual_far))
        )
    ]
    for copy in copies:
        copy.start()
    for copy in copies:
        copy.wait()


def per_device(
    flow_state, point_cell, normals, rbf_weights, block_owner, block_start, stiff_diag, stiff_chord
):
    flow = flow_state.reshape(160, 128)
    weights = rbf_weights.reshape(NBLK * BP, 128)
    owner = block_owner.reshape(1, NBLK)
    start = block_start.reshape(1, NBLK)
    arrays = (flow, point_cell, normals, weights, owner, start, stiff_diag, stiff_chord)
    vmem = pl.BlockSpec(memory_space=pltpu.VMEM)
    far = pl.BlockSpec(memory_space=pltpu.HBM)
    dma = pltpu.SemaphoreType.DMA
    shapes = (
        jax.ShapeDtypeStruct((160, 128), F32),
        jax.ShapeDtypeStruct((3, SPAN, 512), F32),
        jax.ShapeDtypeStruct((3, SPAN, 512), F32),
    )
    results = pl.pallas_call(
        kernel,
        out_shape=shapes,
        in_specs=[far] * 8,
        out_specs=(vmem, vmem, vmem),
        scratch_shapes=[
            pltpu.VMEM((160, 128), F32),
            pltpu.VMEM((NBLK, BP), jnp.int32),
            pltpu.VMEM((3, NBLK, BP), F32),
            pltpu.VMEM((NBLK * BP, 128), BF16),
            pltpu.VMEM((1, NBLK), jnp.int32),
            pltpu.VMEM((1, NBLK), jnp.int32),
            pltpu.VMEM((SPAN, 512), F32),
            pltpu.VMEM((SPAN, 512), F32),
            pltpu.VMEM((8, 128), jnp.int32),
            pltpu.VMEM((8, 128), jnp.int32),
            pltpu.VMEM((3, NBLK, 128), F32),
            pltpu.VMEM((32, 128), F32),
            pltpu.VMEM((NROW, 8, 128), F32),
            pltpu.VMEM((NROW, 8, 128), F32),
            pltpu.VMEM((SPAN, LINE, 128), F32),
            pltpu.VMEM((NX, LINE, 128), F32),
            pltpu.VMEM((LINE, 128), F32),
            pltpu.VMEM((NY, LINE, 128), F32),
            pltpu.VMEM((ROWS, LINE, 128), F32),
            pltpu.VMEM((1, 128), F32),
            pltpu.VMEM((NROW, 1, 128), F32),
            pltpu.VMEM((2, 24, 128), F32),
            pltpu.VMEM((5, 8, 128), F32),
            pltpu.VMEM((5, 8, 128), F32),
            pltpu.VMEM((24, 128), F32),
            pltpu.VMEM((24, 128), F32),
            pltpu.VMEM((SPAN, 8, 128), F32),
            pltpu.VMEM((SPAN, 8, 128), F32),
            pltpu.VMEM((2, 2, 8, 128), F32),
            pltpu.VMEM((2, 2, 8, 128), F32),
            pltpu.VMEM((HALO + 1, SPAN, 16, 128), F32),
            pltpu.VMEM((HALO + 1, 3, SPAN, 512), F32),
            dma((8,)),
            dma((7,)),
            dma((7,)),
            dma((12,)),
            dma((12,)),
            dma((4,)),
            dma((4,)),
        ],
        compiler_params=pltpu.CompilerParams(
            collective_id=0, has_side_effects=True, vmem_limit_bytes=16 * 1024 * 1024
        ),
        cost_estimate=pl.CostEstimate(flops=20_000_000, bytes_accessed=600_000, transcendentals=0),
        name="coupling_step",
    )(*[pltpu.with_memory_space_constraint(array, pltpu.HBM) for array in arrays])
    fluid_next, displacement, residual = pl.pallas_call(
        write_out,
        out_shape=shapes,
        in_specs=[vmem] * 3,
        out_specs=(far, far, far),
        scratch_shapes=[dma((3,))],
        compiler_params=pltpu.CompilerParams(vmem_limit_bytes=1024 * 1024),
        name="write_out",
    )(*[pltpu.with_memory_space_constraint(result, pltpu.VMEM) for result in results])
    return fluid_next.reshape(5, 4, 8, 128), displacement, residual


def solution(mesh):
    return jax.shard_map(
        per_device,
        mesh=mesh,
        in_specs=(
            P(None, "brick", "row", None),
            P(("brick", "row"), None),
            P(None, ("brick", "row"), None),
            P(("brick", "row"), None, None),
            P(("brick", "row"), None),
            P(("brick", "row")),
            P("row", None),
            P("row", None),
        ),
        out_specs=(P(None, "brick", "row", None), P(None, "row", None), P(None, "row", None)),
        check_vma=False,
    )
```

```python
import jax
import jax.numpy as jnp
from jax import lax
from jax.experimental import pallas as pl
from jax.experimental.pallas import tpu as pltpu
from jax.sharding import PartitionSpec as P

NX = 8
NY = 8
NBRICK = NX * NY
NROW = 16
NBLK = 16
BP = 64
SPAN = 8
HALO = 3
ROWS = SPAN + 2 * HALO
LINE = 12
FAR_FIRST = (4, 3, 5, 2, 6, 1, 7)
ROW_FAR_FIRST = (8, 7, 9, 6, 10, 5, 11, 4, 12, 3, 13, 2, 14, 1, 15)
CENTRE = 4.0
WIDTH = 4.0
PRESSURE = 0.4
FLUX = 0.05
SMOOTH = 0.1
MESH = pl.DeviceIdType.MESH
F32 = jnp.float32
BF16 = jnp.bfloat16


def iota(shape, axis):
    return lax.broadcasted_iota(jnp.int32, shape, axis)


def select_rows(chosen, values):
    first = values.astype(BF16)
    second = (values - first.astype(F32)).astype(BF16)
    terms = jnp.concatenate([first, second], axis=1)
    both = jnp.dot(chosen.astype(F32).astype(BF16), terms, preferred_element_type=F32)
    return both[:, 0:128] + both[:, 128:256]


def take_lanes(values, index):
    return jnp.take_along_axis(values, index, axis=1, mode="promise_in_bounds")


def sample_pressure(flow, cell, packed_cell, pressure):
    density = flow[0:32, :]
    inverse = 1.0 / density
    kinetic = jnp.zeros_like(density)
    for c in range(3):
        momentum = flow[32 * (c + 1) : 32 * (c + 2), :]
        kinetic = kinetic + momentum * (momentum * inverse)
    pressure[...] = PRESSURE * (flow[128:160, :] - 0.5 * kinetic)
    packed_cell[:, 0:BP] = cell[0:8, :]
    packed_cell[:, BP:128] = cell[8:16, :]
    index = packed_cell[...]
    high = index >> 7
    low = index & 127
    sampled = jnp.zeros((8, 128), F32)
    for k in range(32):
        line = jnp.broadcast_to(pressure[k : k + 1, :], (8, 128))
        sampled = jnp.where(high == k, take_lanes(line, low), sampled)
    swapped = pltpu.roll(sampled, BP, 1)
    left = iota((8, 128), 1) < BP
    return jnp.concatenate(
        [jnp.where(left, sampled, swapped), jnp.where(left, swapped, sampled)], axis=0
    )


def sort_blocks(owner, start, line_of):
    line_of[0:1, :] = jnp.full((1, 128), -1, jnp.int32)
    line_of[1:2, :] = jnp.zeros((1, 128), jnp.int32)
    line_of[0:1, 0:NBLK] = owner[...]
    line_of[1:2, 0:NBLK] = start[...]
    lane = iota((16, 128), 1).astype(F32)
    named = jnp.broadcast_to(line_of[0:1, :], (16, 128))
    mine = named == iota((16, 128), 0)
    first = jnp.min(jnp.where(mine, lane, 999.0), axis=1, keepdims=True)
    is_first = jnp.sum(jnp.where(mine & (lane == first), 1.0, 0.0), axis=0, keepdims=True)
    key = 2.0 * named[0:1, :].astype(F32) + (1.0 - is_first)
    key = jnp.broadcast_to(key, (128, 128))
    begins = jnp.broadcast_to(line_of[1:2, :].astype(F32), (128, 128))
    row = iota((128, 128), 0)
    wanted = (2 * (row >> 3) + (row & 1)).astype(F32)
    begin = jnp.sum(jnp.where(key == wanted, begins, 0.0), axis=1, keepdims=True)
    key = jnp.where(iota((128, 128), 1) < NBLK, key, -1.0)
    again = jnp.maximum(key, jnp.maximum(shifted(key, 16), shifted(key, 32)))
    component = iota((128, 128), 1) >> 4
    chosen = (again == wanted) & (component == ((row & 7) >> 1))
    return chosen[:, 0:48], jnp.broadcast_to(begin, (128, 128))


def shifted(value, by):
    return jnp.broadcast_to(pltpu.roll(value[0:8], by, 1)[0:1], value.shape)


def pack_windows(sampled, normals, doubled, weights, chosen, begin, send):
    doubled[:, :, 0:BP] = normals[...]
    doubled[:, :, BP:128] = normals[...]
    traction = jnp.concatenate([sampled * doubled[c] for c in range(3)], axis=0)
    block = iota((48, 128), 0) & 15
    half = iota((48, 128), 1) >> 6
    spread = [jnp.where(block == 2 * g + half, traction, 0.0).astype(BF16) for g in range(8)]
    forces = jnp.dot(jnp.concatenate(spread, axis=1), weights[...], preferred_element_type=F32)
    windows = select_rows(chosen, forces)
    index = (iota((128, 128), 1) - (begin.astype(jnp.int32) & 127)) & 127
    sub = iota((8, 128), 0)
    for o in range(NROW):
        part = slice(8 * o, 8 * o + 8)
        turned = take_lanes(windows[part], index[part])
        send[o] = jnp.where(sub < 6, turned, begin[part])


def add_windows(received, dense):
    values = received[...].reshape(128, 128)
    low = jnp.broadcast_to(received[:, 6:7, :], (16, 8, 128)).reshape(128, 128)
    high = jnp.broadcast_to(received[:, 7:8, :], (16, 8, 128)).reshape(128, 128)
    row = iota((128, 128), 0)
    lane = iota((128, 128), 1)
    begin = jnp.where((row & 1) == 0, low, high)
    shift = begin.astype(jnp.int32) & 127
    upright = jnp.sum(jnp.where(row == lane, begin, 0.0), axis=0, keepdims=True)
    line = jnp.broadcast_to(upright.astype(jnp.int32) >> 7, (128, 128))
    component = (lane & 7) >> 1
    fits = (component == ((row >> 2) & 3)) & (component < 3)
    place = 4 * (row >> 4) + (row & 3)
    window = (row & 7) < 6
    here = jnp.where(window & (lane >= shift), values, 0.0)
    after = jnp.where(window & (lane < shift), values, 0.0)
    chosen = jnp.concatenate([fits & (place == line), fits & (place == line + 1)], axis=1)
    total = select_rows(chosen, jnp.concatenate([here, after], axis=0))
    for s in range(SPAN):
        dense[s] = total[16 * s : 16 * s + LINE]


def turn(value, by, axis):
    size = value.shape[axis]
    return pltpu.roll(value, by % size, axis)


def next_node(value):
    turned = turn(value, -1, 1)
    sub = iota((8, 128), 0) & 3
    ahead = jnp.where(sub == 3, turn(turned, 3, 0), turn(turned, -1, 0))
    return jnp.where(iota((8, 128), 1) == 127, ahead, turned)


def node_before(value):
    turned = turn(value, 1, 1)
    sub = iota((8, 128), 0) & 3
    behind = jnp.where(sub == 0, turn(turned, -3, 0), turn(turned, 1, 0))
    return jnp.where(iota((8, 128), 1) == 0, behind, turned)


def pieces_along(state, direction):
    density, energy = state[0], state[4]
    inverse = 1.0 / density
    velocity = [state[1 + c] * inverse for c in range(3)]
    kinetic = state[1] * velocity[0] + state[2] * velocity[1] + state[3] * velocity[2]
    pressure = PRESSURE * (energy - 0.5 * kinetic)
    moving = velocity[direction]
    flux = [state[1 + direction]]
    for c in range(3):
        term = state[1 + c] * moving
        flux.append(term + pressure if c == direction else term)
    flux.append((energy + pressure) * moving)
    ahead = [SMOOTH * s + FLUX * f for s, f in zip(state, flux)]
    behind = [SMOOTH * s - FLUX * f for s, f in zip(state, flux)]
    return ahead, behind


def fluid_step(flow, x_low, x_high, y_low, y_high, result):
    own = [[flow[32 * f + 8 * i : 32 * f + 8 * i + 8, :] for f in range(5)] for i in range(4)]
    total = [[(1.0 - 6.0 * SMOOTH) * own[i][f] for f in range(5)] for i in range(4)]
    slab = [[x_low[f] for f in range(5)]] + own + [[x_high[f] for f in range(5)]]
    for i in range(6):
        ahead, behind = pieces_along(slab[i], 0)
        for f in range(5):
            if i <= 3:
                total[i][f] = total[i][f] + ahead[f]
            if i >= 2:
                total[i - 2][f] = total[i - 2][f] + behind[f]
    from_low, _ = pieces_along([y_low[4 * f : 4 * f + 4, :] for f in range(5)], 1)
    _, from_high = pieces_along([y_high[4 * f : 4 * f + 4, :] for f in range(5)], 1)
    sub = iota((8, 128), 0)
    for i in range(4):
        ahead, behind = pieces_along(own[i], 1)
        for f in range(5):
            low = jnp.broadcast_to(from_low[f][i : i + 1, :], (8, 128))
            high = jnp.broadcast_to(from_high[f][i : i + 1, :], (8, 128))
            total[i][f] = total[i][f] + jnp.where(sub == 0, low, turn(ahead[f], 1, 0))
            total[i][f] = total[i][f] + jnp.where(sub == 7, high, turn(behind[f], -1, 0))
        ahead, behind = pieces_along(own[i], 2)
        for f in range(5):
            total[i][f] = total[i][f] + turn(ahead[f], 1, 1) + turn(behind[f], -1, 1)
            result[32 * f + 8 * i : 32 * f + 8 * i + 8, :] = total[i][f]


def lay_stiffness(source, target):
    for s in range(SPAN):
        for j in range(4):
            line = source[s : s + 1, 128 * j : 128 * j + 128]
            target[s, j : j + 1, :] = line
            target[s, 4 + j : 5 + j, :] = line


def kernel(
    flow_far, cell_far, normals_far, weights_far, owner_far, start_far, diag_far, chord_far,
    fluid_next, displacement, residual,
    flow, cell, normals, weights, owner, start, stiff_diag, stiff_chord,
    packed_cell, line_of, doubled, pressure, windows_out, windows_in, dense, x_in, x_sum, y_in, lines,
    shares_out, shares_in, y_edges, x_low, x_high, y_low, y_high,
    diag_rows, chord_rows, diag_halo, chord_halo, fields, turned,
    load_sem, send_sem, recv_sem, fluid_send, fluid_recv, stiff_send, stiff_recv,
):
    brick = lax.axis_index("brick")
    row = lax.axis_index("row")
    x = lax.div(brick, NY)
    y = lax.rem(brick, NY)
    row_up = lax.rem(row + 1, NROW)
    row_down = lax.rem(row + NROW - 1, NROW)
    brick_up = lax.rem(brick + 1, NBRICK)
    brick_down = lax.rem(brick + NBRICK - 1, NBRICK)

    def x_peer(k):
        return lax.rem(x + k, NX) * NY + y

    def y_peer(k):
        return x * NY + lax.rem(y + k, NY)

    barrier = pltpu.get_barrier_semaphore()

    def greet(to_brick, to_row):
        pl.semaphore_signal(barrier, inc=1, device_id=(to_brick, to_row), device_id_type=MESH)

    for k in ROW_FAR_FIRST:
        greet(brick, lax.rem(row + k, NROW))

    loads = [
        pltpu.make_async_copy(far, near, load_sem.at[n])
        for n, (far, near) in enumerate((
            (flow_far, flow), (cell_far, cell), (weights_far, weights), (normals_far, normals),
            (owner_far, owner), (start_far, start), (diag_far, stiff_diag), (chord_far, stiff_chord),
        ))
    ]
    for load in loads:
        load.start()

    for k in FAR_FIRST:
        greet(x_peer(k), row)
        greet(y_peer(k), row)
    greet(brick_up, row)
    greet(brick_down, row)

    def copy_to(source, target, send, receive, to_brick, to_row):
        return pltpu.make_async_remote_copy(
            src_ref=source, dst_ref=target, send_sem=send, recv_sem=receive,
            device_id=(to_brick, to_row), device_id_type=MESH,
        )

    loads[4].wait()
    loads[5].wait()
    chosen, begin = sort_blocks(owner, start, line_of)
    loads[0].wait()
    loads[1].wait()
    sampled = sample_pressure(flow, cell, packed_cell, pressure)
    loads[2].wait()
    loads[3].wait()
    pack_windows(sampled, normals, doubled, weights, chosen, begin, windows_out)
    y_edges[...] = jnp.zeros((2, 24, 128), F32)
    y_edges[0, 0:20, :] = flow[pl.ds(0, 20, stride=8), :]
    y_edges[1, 0:20, :] = flow[pl.ds(7, 20, stride=8), :]

    pl.semaphore_wait(barrier, (NROW - 1) + 1 * (NX - 1) + (NY - 1) + 2)

    for k in ROW_FAR_FIRST:
        to = lax.rem(row + k, NROW)
        copy_to(windows_out.at[to], windows_in.at[row], send_sem.at[0], recv_sem.at[0], brick, to).start()

    windows_in[row] = windows_out[row]

    fluid_copies = [
        copy_to(y_edges.at[0], y_high, fluid_send.at[0], fluid_recv.at[0], brick, row_down),
        copy_to(y_edges.at[1], y_low, fluid_send.at[1], fluid_recv.at[1], brick, row_up),
    ]
    for f in range(5):
        plane = flow.at[pl.ds(32 * f, 8)]
        fluid_copies.append(
            copy_to(plane, x_high.at[f], fluid_send.at[2 + f], fluid_recv.at[2 + f], brick_down, row)
        )
        plane = flow.at[pl.ds(32 * f + 24, 8)]
        fluid_copies.append(
            copy_to(plane, x_low.at[f], fluid_send.at[7 + f], fluid_recv.at[7 + f], brick_up, row)
        )
    for copy in fluid_copies:
        copy.start()
    loads[6].wait()
    loads[7].wait()
    lay_stiffness(stiff_diag, diag_rows)
    lay_stiffness(stiff_chord, chord_rows)
    stiff_copies = []
    for n, (rows, halo) in enumerate(((diag_rows, diag_halo), (chord_rows, chord_halo))):
        stiff_copies.append(
            copy_to(rows.at[pl.ds(SPAN - 2, 2)], halo.at[0], stiff_send.at[2 * n], stiff_recv.at[2 * n], brick, row_up)
        )
        stiff_copies.append(
            copy_to(rows.at[pl.ds(0, 2)], halo.at[1], stiff_send.at[2 * n + 1], stiff_recv.at[2 * n + 1], brick, row_down)
        )
    for copy in stiff_copies:
        copy.start()

    def await_copies(buffer, count, n):
        part = buffer.at[pl.ds(0, count)]
        copy_to(part, part, send_sem.at[n], recv_sem.at[n], brick_up, row).wait_recv()

    await_copies(windows_in, NROW - 1, 0)
    add_windows(windows_in, dense)

    for k in FAR_FIRST:
        to = lax.rem(x + k, NX)
        copy_to(dense.at[to], x_in.at[x], send_sem.at[1], recv_sem.at[1], x_peer(k), row).start()

    x_in[x] = dense[x]
    await_copies(x_in, NX - 1, 1)
    total = x_in[0]
    for k in range(1, NX):
        total = total + x_in[k]
    x_sum[...] = total

    for k in FAR_FIRST:
        copy_to(x_sum, y_in.at[y], send_sem.at[2], recv_sem.at[2], y_peer(k), row).start()

    y_in[y] = total

    for copy in fluid_copies:
        copy.wait_recv()
    fluid_step(flow, x_low, x_high, y_low, y_high, fluid_next)
    for copy in stiff_copies:
        copy.wait_recv()

    await_copies(y_in, NY - 1, 2)
    total = y_in[0]
    for k in range(1, NY):
        total = total + y_in[k]
    lines[HALO + x] = total

    own_line = lines.at[HALO + x]

    goes_up = (x >= SPAN - HALO) & (row < NROW - 1)
    goes_down = (x < HALO) & (row > 0)

    def send_beside(steps):
        @pl.when(goes_up)
        def _():
            for k in steps:
                target = lines.at[x - (SPAN - HALO)]
                copy_to(own_line, target, send_sem.at[4], recv_sem.at[4], x_peer(k), row_up).start()

        @pl.when(goes_down)
        def _():
            for k in steps:
                target = lines.at[HALO + SPAN + x]
                copy_to(own_line, target, send_sem.at[5], recv_sem.at[5], x_peer(k), row_down).start()

    send_beside((4, 3, 5))
    for k in FAR_FIRST:
        copy_to(own_line, own_line, send_sem.at[3], recv_sem.at[3], x_peer(k), row).start()
    send_beside((2, 6, 1, 7, 0))

    @pl.when(row == 0)
    def _():
        lines[0:HALO] = jnp.zeros((HALO, LINE, 128), F32)

    @pl.when(row == NROW - 1)
    def _():
        lines[HALO + SPAN : ROWS] = jnp.zeros((HALO, LINE, 128), F32)

    await_copies(lines, NX - 1, 3)

    @pl.when(row > 0)
    def _():
        await_copies(lines, HALO, 4)

    @pl.when(row < NROW - 1)
    def _():
        await_copies(lines, HALO, 5)

    below = jnp.where(row > 0, 1.0, 0.0).astype(F32)
    above = jnp.where(row < NROW - 1, 1.0, 0.0).astype(F32)
    diag = [None, diag_halo[0, 0], diag_halo[0, 1]] + [diag_rows[s] for s in range(SPAN)]
    diag = diag + [diag_halo[1, 0], diag_halo[1, 1]]
    chord = [None, chord_halo[0, 0], chord_halo[0, 1]] + [chord_rows[s] for s in range(SPAN)]
    chord = chord + [chord_halo[1, 0], chord_halo[1, 1]]
    diag = [None if d is None else (d + (2.0 - CENTRE)) * (1.0 / WIDTH) for d in diag]
    chord = [None if d is None else d * (1.0 / WIDTH) for d in chord]
    products = [jnp.zeros((8, 128), F32) for _ in range(6)]
    for half in range(2):
        part = slice(8 * half, 8 * half + 8)
        if half == 0:
            levels = [[lines[i, 0:8, :] for i in range(ROWS)]]
        else:
            spare = jnp.zeros((4, 128), F32)
            levels = [[jnp.concatenate([lines[i, 8:LINE, :], spare], axis=0) for i in range(ROWS)]]
        for level in range(1, HALO + 1):
            before = levels[-1]
            after = [None] * ROWS
            for i in range(level, ROWS - level):
                flow_on = chord[i] * (before[i] - next_node(before[i]))
                value = diag[i] * before[i] + (flow_on - node_before(flow_on))
                value = value - (1.0 / WIDTH) * (before[i - 1] + before[i + 1])
                if i < HALO:
                    value = value * below
                if i >= HALO + SPAN:
                    value = value * above
                after[i] = value
            levels.append(after)
        for i in range(HALO, HALO + SPAN):
            for level in range(HALO + 1):
                fields[level, i - HALO, part, :] = levels[level][i]
            for n, (p, q) in enumerate(((0, 0), (0, 1), (1, 1), (1, 2), (2, 2), (2, 3))):
                products[n] = products[n] + levels[p][i] * levels[q][i]
    share = jnp.zeros((1, 128), F32)
    lane = iota((1, 128), 1)
    for n in range(6):
        inner = jnp.sum(jnp.sum(products[n], axis=0, keepdims=True), axis=1, keepdims=True)
        share = jnp.where(lane == n, jnp.broadcast_to(inner, (1, 128)), share)
    shares_out[...] = share

    for k in ROW_FAR_FIRST:
        to = lax.rem(row + k, NROW)
        copy_to(shares_out, shares_in.at[row], send_sem.at[6], recv_sem.at[6], brick, to).start()

    shares_in[row] = shares_out[...]

    for level in range(HALO + 1):
        for s in range(SPAN):
            for c in range(3):
                for j in range(4):
                    line = fields[level, s, 4 * c + j : 4 * c + j + 1, :]
                    turned[level, c, s : s + 1, 128 * j : 128 * j + 128] = line

    await_copies(shares_in, NROW - 1, 6)
    share = shares_in[0]
    for k in range(1, NROW):
        share = share + shares_in[k]
    moment = [jnp.broadcast_to(share[:, n : n + 1], (8, 128)) for n in range(6)]
    matrix = [CENTRE * moment[n] + WIDTH * moment[n + 1] for n in range(5)]
    m00, m01, m02, m11, m12, m22 = matrix[0], matrix[1], matrix[2], matrix[2], matrix[3], matrix[4]
    l10 = m01 / m00
    l20 = m02 / m00
    d1 = m11 - l10 * m01
    e = m12 - l10 * m02
    l21 = e / d1
    d2 = m22 - l20 * m02 - l21 * e
    y1 = moment[1] - l10 * moment[0]
    y2 = moment[2] - l20 * moment[0] - l21 * y1
    w2 = y2 / d2
    w1 = y1 / d1 - l21 * w2
    w0 = moment[0] / m00 - l10 * w1 - l20 * w2
    r0 = 1.0 - CENTRE * w0
    r1 = -(WIDTH * w0 + CENTRE * w1)
    r2 = -(WIDTH * w1 + CENTRE * w2)
    r3 = -(WIDTH * w2)
    for c in range(3):
        for j in range(4):
            part = slice(128 * j, 128 * j + 128)
            v = [turned[level, c, :, part] for level in range(4)]
            displacement[c, :, part] = w0 * v[0] + w1 * v[1] + w2 * v[2]
            residual[c, :, part] = (r0 * v[0] + r1 * v[1]) + (r2 * v[2] + r3 * v[3])

    def await_sent(buffer, count, n):
        part = buffer.at[pl.ds(0, count)]
        copy_to(part, part, send_sem.at[n], recv_sem.at[n], brick_up, row).wait_send()

    await_sent(windows_in, NROW - 1, 0)
    await_sent(x_in, NX - 1, 1)
    await_sent(y_in, NY - 1, 2)
    await_sent(lines, NX - 1, 3)

    @pl.when(goes_up)
    def _():
        await_sent(lines, NX, 4)

    @pl.when(goes_down)
    def _():
        await_sent(lines, NX, 5)

    await_sent(shares_in, NROW - 1, 6)
    for copy in fluid_copies + stiff_copies:
        copy.wait_send()


def write_out(fluid, displacement, residual, fluid_far, displacement_far, residual_far, sem):
    copies = [
        pltpu.make_async_copy(near, far, sem.at[n])
        for n, (near, far) in enumerate(
            ((fluid, fluid_far), (displacement, displacement_far), (residual, residual_far))
        )
    ]
    for copy in copies:
        copy.start()
    for copy in copies:
        copy.wait()


def per_device(
    flow_state, point_cell, normals, rbf_weights, block_owner, block_start, stiff_diag, stiff_chord
):
    flow = flow_state.reshape(160, 128)
    weights = rbf_weights.reshape(NBLK * BP, 128)
    owner = block_owner.reshape(1, NBLK)
    start = block_start.reshape(1, NBLK)
    arrays = (flow, point_cell, normals, weights, owner, start, stiff_diag, stiff_chord)
    vmem = pl.BlockSpec(memory_space=pltpu.VMEM)
    far = pl.BlockSpec(memory_space=pltpu.HBM)
    dma = pltpu.SemaphoreType.DMA
    shapes = (
        jax.ShapeDtypeStruct((160, 128), F32),
        jax.ShapeDtypeStruct((3, SPAN, 512), F32),
        jax.ShapeDtypeStruct((3, SPAN, 512), F32),
    )
    results = pl.pallas_call(
        kernel,
        out_shape=shapes,
        in_specs=[far] * 8,
        out_specs=(vmem, vmem, vmem),
        scratch_shapes=[
            pltpu.VMEM((160, 128), F32),
            pltpu.VMEM((NBLK, BP), jnp.int32),
            pltpu.VMEM((3, NBLK, BP), F32),
            pltpu.VMEM((NBLK * BP, 128), BF16),
            pltpu.VMEM((1, NBLK), jnp.int32),
            pltpu.VMEM((1, NBLK), jnp.int32),
            pltpu.VMEM((SPAN, 512), F32),
            pltpu.VMEM((SPAN, 512), F32),
            pltpu.VMEM((8, 128), jnp.int32),
            pltpu.VMEM((8, 128), jnp.int32),
            pltpu.VMEM((3, NBLK, 128), F32),
            pltpu.VMEM((32, 128), F32),
            pltpu.VMEM((NROW, 8, 128), F32),
            pltpu.VMEM((NROW, 8, 128), F32),
            pltpu.VMEM((SPAN, LINE, 128), F32),
            pltpu.VMEM((NX, LINE, 128), F32),
            pltpu.VMEM((LINE, 128), F32),
            pltpu.VMEM((NY, LINE, 128), F32),
            pltpu.VMEM((ROWS, LINE, 128), F32),
            pltpu.VMEM((1, 128), F32),
            pltpu.VMEM((NROW, 1, 128), F32),
            pltpu.VMEM((2, 24, 128), F32),
            pltpu.VMEM((5, 8, 128), F32),
            pltpu.VMEM((5, 8, 128), F32),
            pltpu.VMEM((24, 128), F32),
            pltpu.VMEM((24, 128), F32),
            pltpu.VMEM((SPAN, 8, 128), F32),
            pltpu.VMEM((SPAN, 8, 128), F32),
            pltpu.VMEM((2, 2, 8, 128), F32),
            pltpu.VMEM((2, 2, 8, 128), F32),
            pltpu.VMEM((HALO + 1, SPAN, 16, 128), F32),
            pltpu.VMEM((HALO + 1, 3, SPAN, 512), F32),
            dma((8,)),
            dma((7,)),
            dma((7,)),
            dma((12,)),
            dma((12,)),
            dma((4,)),
            dma((4,)),
        ],
        compiler_params=pltpu.CompilerParams(
            collective_id=0, has_side_effects=True, vmem_limit_bytes=16 * 1024 * 1024
        ),
        cost_estimate=pl.CostEstimate(flops=20_000_000, bytes_accessed=600_000, transcendentals=0),
        name="coupling_step",
    )(*[pltpu.with_memory_space_constraint(array, pltpu.HBM) for array in arrays])
    fluid_next, displacement, residual = pl.pallas_call(
        write_out,
        out_shape=shapes,
        in_specs=[vmem] * 3,
        out_specs=(far, far, far),
        scratch_shapes=[dma((3,))],
        compiler_params=pltpu.CompilerParams(vmem_limit_bytes=1024 * 1024),
        name="write_out",
    )(*[pltpu.with_memory_space_constraint(result, pltpu.VMEM) for result in results])
    return fluid_next.reshape(5, 4, 8, 128), displacement, residual


def solution(mesh):
    return jax.shard_map(
        per_device,
        mesh=mesh,
        in_specs=(
            P(None, "brick", "row", None),
            P(("brick", "row"), None),
            P(None, ("brick", "row"), None),
            P(("brick", "row"), None, None),
            P(("brick", "row"), None),
            P(("brick", "row")),
            P("row", None),
            P("row", None),
        ),
        out_specs=(P(None, "brick", "row", None), P(None, "row", None), P(None, "row", None)),
        check_vma=False,
    )
```

```python
import jax
import jax.numpy as jnp
from jax import lax
from jax.experimental import pallas as pl
from jax.experimental.pallas import tpu as pltpu
from jax.sharding import PartitionSpec as P

NX = 8
NY = 8
NBRICK = NX * NY
NROW = 16
NBLK = 16
BP = 64
SPAN = 8
HALO = 3
ROWS = SPAN + 2 * HALO
LINE = 12
FAR_FIRST = (4, 3, 5, 2, 6, 1, 7)
ROW_FAR_FIRST = (8, 7, 9, 6, 10, 5, 11, 4, 12, 3, 13, 2, 14, 1, 15)
CENTRE = 4.0
WIDTH = 4.0
PRESSURE = 0.4
FLUX = 0.05
SMOOTH = 0.1
MESH = pl.DeviceIdType.MESH
F32 = jnp.float32
BF16 = jnp.bfloat16


def iota(shape, axis):
    return lax.broadcasted_iota(jnp.int32, shape, axis)


def select_rows(chosen, values):
    first = values.astype(BF16)
    second = (values - first.astype(F32)).astype(BF16)
    terms = jnp.concatenate([first, second], axis=1)
    both = jnp.dot(chosen.astype(F32).astype(BF16), terms, preferred_element_type=F32)
    return both[:, 0:128] + both[:, 128:256]


def take_lanes(values, index):
    return jnp.take_along_axis(values, index, axis=1, mode="promise_in_bounds")


def sample_pressure(flow, cell, packed_cell, pressure):
    density = flow[0:32, :]
    inverse = 1.0 / density
    kinetic = jnp.zeros_like(density)
    for c in range(3):
        momentum = flow[32 * (c + 1) : 32 * (c + 2), :]
        kinetic = kinetic + momentum * (momentum * inverse)
    pressure[...] = PRESSURE * (flow[128:160, :] - 0.5 * kinetic)
    packed_cell[:, 0:BP] = cell[0:8, :]
    packed_cell[:, BP:128] = cell[8:16, :]
    index = packed_cell[...]
    high = index >> 7
    low = index & 127
    sampled = jnp.zeros((8, 128), F32)
    for k in range(32):
        line = jnp.broadcast_to(pressure[k : k + 1, :], (8, 128))
        sampled = jnp.where(high == k, take_lanes(line, low), sampled)
    swapped = pltpu.roll(sampled, BP, 1)
    left = iota((8, 128), 1) < BP
    return jnp.concatenate(
        [jnp.where(left, sampled, swapped), jnp.where(left, swapped, sampled)], axis=0
    )


def sort_blocks(owner, start, line_of):
    line_of[0:1, :] = jnp.full((1, 128), -1, jnp.int32)
    line_of[1:2, :] = jnp.zeros((1, 128), jnp.int32)
    line_of[0:1, 0:NBLK] = owner[...]
    line_of[1:2, 0:NBLK] = start[...]
    lane = iota((16, 128), 1).astype(F32)
    named = jnp.broadcast_to(line_of[0:1, :], (16, 128))
    mine = named == iota((16, 128), 0)
    first = jnp.min(jnp.where(mine, lane, 999.0), axis=1, keepdims=True)
    is_first = jnp.sum(jnp.where(mine & (lane == first), 1.0, 0.0), axis=0, keepdims=True)
    key = 2.0 * named[0:1, :].astype(F32) + (1.0 - is_first)
    key = jnp.broadcast_to(key, (128, 128))
    begins = jnp.broadcast_to(line_of[1:2, :].astype(F32), (128, 128))
    row = iota((128, 128), 0)
    wanted = (2 * (row >> 3) + (row & 1)).astype(F32)
    begin = jnp.sum(jnp.where(key == wanted, begins, 0.0), axis=1, keepdims=True)
    key = jnp.where(iota((128, 128), 1) < NBLK, key, -1.0)
    again = jnp.maximum(key, jnp.maximum(shifted(key, 16), shifted(key, 32)))
    component = iota((128, 128), 1) >> 4
    chosen = (again == wanted) & (component == ((row & 7) >> 1))
    return chosen[:, 0:48], jnp.broadcast_to(begin, (128, 128))


def shifted(value, by):
    return jnp.broadcast_to(pltpu.roll(value[0:8], by, 1)[0:1], value.shape)


def pack_windows(sampled, normals, doubled, weights, chosen, begin, send):
    doubled[:, :, 0:BP] = normals[...]
    doubled[:, :, BP:128] = normals[...]
    traction = jnp.concatenate([sampled * doubled[c] for c in range(3)], axis=0)
    block = iota((48, 128), 0) & 15
    half = iota((48, 128), 1) >> 6
    spread = [jnp.where(block == 2 * g + half, traction, 0.0).astype(BF16) for g in range(8)]
    forces = jnp.dot(jnp.concatenate(spread, axis=1), weights[...], preferred_element_type=F32)
    windows = select_rows(chosen, forces)
    index = (iota((128, 128), 1) - (begin.astype(jnp.int32) & 127)) & 127
    sub = iota((8, 128), 0)
    for o in range(NROW):
        part = slice(8 * o, 8 * o + 8)
        turned = take_lanes(windows[part], index[part])
        send[o] = jnp.where(sub < 6, turned, begin[part])


def add_windows(received, dense):
    values = received[...].reshape(128, 128)
    low = jnp.broadcast_to(received[:, 6:7, :], (16, 8, 128)).reshape(128, 128)
    high = jnp.broadcast_to(received[:, 7:8, :], (16, 8, 128)).reshape(128, 128)
    row = iota((128, 128), 0)
    lane = iota((128, 128), 1)
    begin = jnp.where((row & 1) == 0, low, high)
    shift = begin.astype(jnp.int32) & 127
    upright = jnp.sum(jnp.where(row == lane, begin, 0.0), axis=0, keepdims=True)
    line = jnp.broadcast_to(upright.astype(jnp.int32) >> 7, (128, 128))
    component = (lane & 7) >> 1
    fits = (component == ((row >> 2) & 3)) & (component < 3)
    place = 4 * (row >> 4) + (row & 3)
    window = (row & 7) < 6
    here = jnp.where(window & (lane >= shift), values, 0.0)
    after = jnp.where(window & (lane < shift), values, 0.0)
    chosen = jnp.concatenate([fits & (place == line), fits & (place == line + 1)], axis=1)
    total = select_rows(chosen, jnp.concatenate([here, after], axis=0))
    for s in range(SPAN):
        dense[s] = total[16 * s : 16 * s + LINE]


def turn(value, by, axis):
    size = value.shape[axis]
    return pltpu.roll(value, by % size, axis)


def next_node(value):
    turned = turn(value, -1, 1)
    sub = iota((8, 128), 0) & 3
    ahead = jnp.where(sub == 3, turn(turned, 3, 0), turn(turned, -1, 0))
    return jnp.where(iota((8, 128), 1) == 127, ahead, turned)


def node_before(value):
    turned = turn(value, 1, 1)
    sub = iota((8, 128), 0) & 3
    behind = jnp.where(sub == 0, turn(turned, -3, 0), turn(turned, 1, 0))
    return jnp.where(iota((8, 128), 1) == 0, behind, turned)


def pieces_along(state, direction):
    density, energy = state[0], state[4]
    inverse = 1.0 / density
    velocity = [state[1 + c] * inverse for c in range(3)]
    kinetic = state[1] * velocity[0] + state[2] * velocity[1] + state[3] * velocity[2]
    pressure = PRESSURE * (energy - 0.5 * kinetic)
    moving = velocity[direction]
    flux = [state[1 + direction]]
    for c in range(3):
        term = state[1 + c] * moving
        flux.append(term + pressure if c == direction else term)
    flux.append((energy + pressure) * moving)
    ahead = [SMOOTH * s + FLUX * f for s, f in zip(state, flux)]
    behind = [SMOOTH * s - FLUX * f for s, f in zip(state, flux)]
    return ahead, behind


def fluid_step(flow, x_low, x_high, y_low, y_high, result):
    own = [[flow[32 * f + 8 * i : 32 * f + 8 * i + 8, :] for f in range(5)] for i in range(4)]
    total = [[(1.0 - 6.0 * SMOOTH) * own[i][f] for f in range(5)] for i in range(4)]
    slab = [[x_low[f] for f in range(5)]] + own + [[x_high[f] for f in range(5)]]
    for i in range(6):
        ahead, behind = pieces_along(slab[i], 0)
        for f in range(5):
            if i <= 3:
                total[i][f] = total[i][f] + ahead[f]
            if i >= 2:
                total[i - 2][f] = total[i - 2][f] + behind[f]
    from_low, _ = pieces_along([y_low[4 * f : 4 * f + 4, :] for f in range(5)], 1)
    _, from_high = pieces_along([y_high[4 * f : 4 * f + 4, :] for f in range(5)], 1)
    sub = iota((8, 128), 0)
    for i in range(4):
        ahead, behind = pieces_along(own[i], 1)
        for f in range(5):
            low = jnp.broadcast_to(from_low[f][i : i + 1, :], (8, 128))
            high = jnp.broadcast_to(from_high[f][i : i + 1, :], (8, 128))
            total[i][f] = total[i][f] + jnp.where(sub == 0, low, turn(ahead[f], 1, 0))
            total[i][f] = total[i][f] + jnp.where(sub == 7, high, turn(behind[f], -1, 0))
        ahead, behind = pieces_along(own[i], 2)
        for f in range(5):
            total[i][f] = total[i][f] + turn(ahead[f], 1, 1) + turn(behind[f], -1, 1)
            result[32 * f + 8 * i : 32 * f + 8 * i + 8, :] = total[i][f]


def lay_stiffness(source, target):
    for s in range(SPAN):
        for j in range(4):
            line = source[s : s + 1, 128 * j : 128 * j + 128]
            target[s, j : j + 1, :] = line
            target[s, 4 + j : 5 + j, :] = line


def kernel(
    flow_far, cell_far, normals_far, weights_far, owner_far, start_far, diag_far, chord_far,
    fluid_next, displacement, residual,
    flow, cell, normals, weights, owner, start, stiff_diag, stiff_chord,
    packed_cell, line_of, doubled, pressure, windows_out, windows_in, dense, x_in, x_sum, y_in, lines,
    shares_out, shares_in, y_edges, x_low, x_high, y_low, y_high,
    diag_rows, chord_rows, diag_halo, chord_halo, fields, turned,
    reach, load_sem, send_sem, recv_sem, fluid_send, fluid_recv, stiff_send, stiff_recv,
):
    brick = lax.axis_index("brick")
    row = lax.axis_index("row")
    x = lax.div(brick, NY)
    y = lax.rem(brick, NY)
    row_up = lax.rem(row + 1, NROW)
    row_down = lax.rem(row + NROW - 1, NROW)
    brick_up = lax.rem(brick + 1, NBRICK)
    brick_down = lax.rem(brick + NBRICK - 1, NBRICK)

    def x_peer(k):
        return lax.rem(x + k, NX) * NY + y

    def y_peer(k):
        return x * NY + lax.rem(y + k, NY)

    barrier = pltpu.get_barrier_semaphore()

    def greet(to_brick, to_row):
        pl.semaphore_signal(barrier, inc=1, device_id=(to_brick, to_row), device_id_type=MESH)

    for k in ROW_FAR_FIRST:
        greet(brick, lax.rem(row + k, NROW))

    loads = [
        pltpu.make_async_copy(far, near, load_sem.at[n])
        for n, (far, near) in enumerate((
            (flow_far, flow), (cell_far, cell), (weights_far, weights), (normals_far, normals),
            (owner_far, owner), (start_far, start), (diag_far, stiff_diag), (chord_far, stiff_chord),
        ))
    ]
    for load in loads:
        load.start()

    near = ((x_peer(1), row), (x_peer(NX - 1), row), (y_peer(1), row), (y_peer(NY - 1), row))
    for to in near + ((brick_up, row), (brick_down, row)):
        greet(*to)

    def copy_to(source, target, send, receive, to_brick, to_row):
        return pltpu.make_async_remote_copy(
            src_ref=source, dst_ref=target, send_sem=send, recv_sem=receive,
            device_id=(to_brick, to_row), device_id_type=MESH,
        )

    loads[4].wait()
    loads[5].wait()
    chosen, begin = sort_blocks(owner, start, line_of)
    loads[0].wait()
    loads[1].wait()
    sampled = sample_pressure(flow, cell, packed_cell, pressure)
    loads[2].wait()
    loads[3].wait()
    pack_windows(sampled, normals, doubled, weights, chosen, begin, windows_out)
    y_edges[...] = jnp.zeros((2, 24, 128), F32)
    y_edges[0, 0:20, :] = flow[pl.ds(0, 20, stride=8), :]
    y_edges[1, 0:20, :] = flow[pl.ds(7, 20, stride=8), :]

    pl.semaphore_wait(barrier, (NROW - 1) + 6)

    def tell(semaphore, to):
        pl.semaphore_signal(semaphore, inc=1, device_id=to, device_id_type=MESH)

    for k in ROW_FAR_FIRST:
        to = lax.rem(row + k, NROW)
        copy_to(windows_out.at[to], windows_in.at[row], send_sem.at[0], recv_sem.at[0], brick, to).start()

    windows_in[row] = windows_out[row]

    for n, to in enumerate(near):
        tell(reach.at[n // 2], to)

    fluid_copies = [
        copy_to(y_edges.at[0], y_high, fluid_send.at[0], fluid_recv.at[0], brick, row_down),
        copy_to(y_edges.at[1], y_low, fluid_send.at[1], fluid_recv.at[1], brick, row_up),
    ]
    for f in range(5):
        plane = flow.at[pl.ds(32 * f, 8)]
        fluid_copies.append(
            copy_to(plane, x_high.at[f], fluid_send.at[2 + f], fluid_recv.at[2 + f], brick_down, row)
        )
        plane = flow.at[pl.ds(32 * f + 24, 8)]
        fluid_copies.append(
            copy_to(plane, x_low.at[f], fluid_send.at[7 + f], fluid_recv.at[7 + f], brick_up, row)
        )
    for copy in fluid_copies:
        copy.start()
    loads[6].wait()
    loads[7].wait()
    lay_stiffness(stiff_diag, diag_rows)
    lay_stiffness(stiff_chord, chord_rows)
    stiff_copies = []
    for n, (rows, halo) in enumerate(((diag_rows, diag_halo), (chord_rows, chord_halo))):
        stiff_copies.append(
            copy_to(rows.at[pl.ds(SPAN - 2, 2)], halo.at[0], stiff_send.at[2 * n], stiff_recv.at[2 * n], brick, row_up)
        )
        stiff_copies.append(
            copy_to(rows.at[pl.ds(0, 2)], halo.at[1], stiff_send.at[2 * n + 1], stiff_recv.at[2 * n + 1], brick, row_down)
        )
    for copy in stiff_copies:
        copy.start()

    for axis in range(2):
        pl.semaphore_wait(reach.at[axis], 2)
    for n, to in enumerate(((x_peer(2), row), (x_peer(NX - 2), row), (y_peer(2), row), (y_peer(NY - 2), row))):
        tell(reach.at[2 + n // 2], to)

    def await_copies(buffer, count, n):
        part = buffer.at[pl.ds(0, count)]
        copy_to(part, part, send_sem.at[n], recv_sem.at[n], brick_up, row).wait_recv()

    await_copies(windows_in, NROW - 1, 0)
    add_windows(windows_in, dense)

    pl.semaphore_wait(reach.at[2], 2)

    for k in FAR_FIRST:
        to = lax.rem(x + k, NX)
        copy_to(dense.at[to], x_in.at[x], send_sem.at[1], recv_sem.at[1], x_peer(k), row).start()

    x_in[x] = dense[x]
    await_copies(x_in, NX - 1, 1)
    total = x_in[0]
    for k in range(1, NX):
        total = total + x_in[k]
    x_sum[...] = total

    pl.semaphore_wait(reach.at[3], 2)

    for k in FAR_FIRST:
        copy_to(x_sum, y_in.at[y], send_sem.at[2], recv_sem.at[2], y_peer(k), row).start()

    y_in[y] = total

    for copy in fluid_copies:
        copy.wait_recv()
    fluid_step(flow, x_low, x_high, y_low, y_high, fluid_next)
    for copy in stiff_copies:
        copy.wait_recv()

    await_copies(y_in, NY - 1, 2)
    total = y_in[0]
    for k in range(1, NY):
        total = total + y_in[k]
    lines[HALO + x] = total

    own_line = lines.at[HALO + x]

    goes_up = (x >= SPAN - HALO) & (row < NROW - 1)
    goes_down = (x < HALO) & (row > 0)

    def send_beside(steps):
        @pl.when(goes_up)
        def _():
            for k in steps:
                target = lines.at[x - (SPAN - HALO)]
                copy_to(own_line, target, send_sem.at[4], recv_sem.at[4], x_peer(k), row_up).start()

        @pl.when(goes_down)
        def _():
            for k in steps:
                target = lines.at[HALO + SPAN + x]
                copy_to(own_line, target, send_sem.at[5], recv_sem.at[5], x_peer(k), row_down).start()

    send_beside((4, 3, 5))
    for k in FAR_FIRST:
        copy_to(own_line, own_line, send_sem.at[3], recv_sem.at[3], x_peer(k), row).start()
    send_beside((2, 6, 1, 7, 0))

    @pl.when(row == 0)
    def _():
        lines[0:HALO] = jnp.zeros((HALO, LINE, 128), F32)

    @pl.when(row == NROW - 1)
    def _():
        lines[HALO + SPAN : ROWS] = jnp.zeros((HALO, LINE, 128), F32)

    await_copies(lines, NX - 1, 3)

    @pl.when(row > 0)
    def _():
        await_copies(lines, HALO, 4)

    @pl.when(row < NROW - 1)
    def _():
        await_copies(lines, HALO, 5)

    below = jnp.where(row > 0, 1.0, 0.0).astype(F32)
    above = jnp.where(row < NROW - 1, 1.0, 0.0).astype(F32)
    diag = [None, diag_halo[0, 0], diag_halo[0, 1]] + [diag_rows[s] for s in range(SPAN)]
    diag = diag + [diag_halo[1, 0], diag_halo[1, 1]]
    chord = [None, chord_halo[0, 0], chord_halo[0, 1]] + [chord_rows[s] for s in range(SPAN)]
    chord = chord + [chord_halo[1, 0], chord_halo[1, 1]]
    diag = [None if d is None else (d + (2.0 - CENTRE)) * (1.0 / WIDTH) for d in diag]
    chord = [None if d is None else d * (1.0 / WIDTH) for d in chord]
    products = [jnp.zeros((8, 128), F32) for _ in range(6)]
    for half in range(2):
        part = slice(8 * half, 8 * half + 8)
        if half == 0:
            levels = [[lines[i, 0:8, :] for i in range(ROWS)]]
        else:
            spare = jnp.zeros((4, 128), F32)
            levels = [[jnp.concatenate([lines[i, 8:LINE, :], spare], axis=0) for i in range(ROWS)]]
        for level in range(1, HALO + 1):
            before = levels[-1]
            after = [None] * ROWS
            for i in range(level, ROWS - level):
                flow_on = chord[i] * (before[i] - next_node(before[i]))
                value = diag[i] * before[i] + (flow_on - node_before(flow_on))
                value = value - (1.0 / WIDTH) * (before[i - 1] + before[i + 1])
                if i < HALO:
                    value = value * below
                if i >= HALO + SPAN:
                    value = value * above
                after[i] = value
            levels.append(after)
        for i in range(HALO, HALO + SPAN):
            for level in range(HALO + 1):
                fields[level, i - HALO, part, :] = levels[level][i]
            for n, (p, q) in enumerate(((0, 0), (0, 1), (1, 1), (1, 2), (2, 2), (2, 3))):
                products[n] = products[n] + levels[p][i] * levels[q][i]
    share = jnp.zeros((1, 128), F32)
    lane = iota((1, 128), 1)
    for n in range(6):
        inner = jnp.sum(jnp.sum(products[n], axis=0, keepdims=True), axis=1, keepdims=True)
        share = jnp.where(lane == n, jnp.broadcast_to(inner, (1, 128)), share)
    shares_out[...] = share

    for k in ROW_FAR_FIRST:
        to = lax.rem(row + k, NROW)
        copy_to(shares_out, shares_in.at[row], send_sem.at[6], recv_sem.at[6], brick, to).start()

    shares_in[row] = shares_out[...]

    for level in range(HALO + 1):
        for s in range(SPAN):
            for c in range(3):
                for j in range(4):
                    line = fields[level, s, 4 * c + j : 4 * c + j + 1, :]
                    turned[level, c, s : s + 1, 128 * j : 128 * j + 128] = line

    await_copies(shares_in, NROW - 1, 6)
    share = shares_in[0]
    for k in range(1, NROW):
        share = share + shares_in[k]
    moment = [jnp.broadcast_to(share[:, n : n + 1], (8, 128)) for n in range(6)]
    matrix = [CENTRE * moment[n] + WIDTH * moment[n + 1] for n in range(5)]
    m00, m01, m02, m11, m12, m22 = matrix[0], matrix[1], matrix[2], matrix[2], matrix[3], matrix[4]
    l10 = m01 / m00
    l20 = m02 / m00
    d1 = m11 - l10 * m01
    e = m12 - l10 * m02
    l21 = e / d1
    d2 = m22 - l20 * m02 - l21 * e
    y1 = moment[1] - l10 * moment[0]
    y2 = moment[2] - l20 * moment[0] - l21 * y1
    w2 = y2 / d2
    w1 = y1 / d1 - l21 * w2
    w0 = moment[0] / m00 - l10 * w1 - l20 * w2
    r0 = 1.0 - CENTRE * w0
    r1 = -(WIDTH * w0 + CENTRE * w1)
    r2 = -(WIDTH * w1 + CENTRE * w2)
    r3 = -(WIDTH * w2)
    for c in range(3):
        for j in range(4):
            part = slice(128 * j, 128 * j + 128)
            v = [turned[level, c, :, part] for level in range(4)]
            displacement[c, :, part] = w0 * v[0] + w1 * v[1] + w2 * v[2]
            residual[c, :, part] = (r0 * v[0] + r1 * v[1]) + (r2 * v[2] + r3 * v[3])

    def await_sent(buffer, count, n):
        part = buffer.at[pl.ds(0, count)]
        copy_to(part, part, send_sem.at[n], recv_sem.at[n], brick_up, row).wait_send()

    await_sent(windows_in, NROW - 1, 0)
    await_sent(x_in, NX - 1, 1)
    await_sent(y_in, NY - 1, 2)
    await_sent(lines, NX - 1, 3)

    @pl.when(goes_up)
    def _():
        await_sent(lines, NX, 4)

    @pl.when(goes_down)
    def _():
        await_sent(lines, NX, 5)

    await_sent(shares_in, NROW - 1, 6)
    for copy in fluid_copies + stiff_copies:
        copy.wait_send()


def write_out(fluid, displacement, residual, fluid_far, displacement_far, residual_far, sem):
    copies = [
        pltpu.make_async_copy(near, far, sem.at[n])
        for n, (near, far) in enumerate(
            ((fluid, fluid_far), (displacement, displacement_far), (residual, residual_far))
        )
    ]
    for copy in copies:
        copy.start()
    for copy in copies:
        copy.wait()


def per_device(
    flow_state, point_cell, normals, rbf_weights, block_owner, block_start, stiff_diag, stiff_chord
):
    flow = flow_state.reshape(160, 128)
    weights = rbf_weights.reshape(NBLK * BP, 128)
    owner = block_owner.reshape(1, NBLK)
    start = block_start.reshape(1, NBLK)
    arrays = (flow, point_cell, normals, weights, owner, start, stiff_diag, stiff_chord)
    vmem = pl.BlockSpec(memory_space=pltpu.VMEM)
    far = pl.BlockSpec(memory_space=pltpu.HBM)
    dma = pltpu.SemaphoreType.DMA
    shapes = (
        jax.ShapeDtypeStruct((160, 128), F32),
        jax.ShapeDtypeStruct((3, SPAN, 512), F32),
        jax.ShapeDtypeStruct((3, SPAN, 512), F32),
    )
    results = pl.pallas_call(
        kernel,
        out_shape=shapes,
        in_specs=[far] * 8,
        out_specs=(vmem, vmem, vmem),
        scratch_shapes=[
            pltpu.VMEM((160, 128), F32),
            pltpu.VMEM((NBLK, BP), jnp.int32),
            pltpu.VMEM((3, NBLK, BP), F32),
            pltpu.VMEM((NBLK * BP, 128), BF16),
            pltpu.VMEM((1, NBLK), jnp.int32),
            pltpu.VMEM((1, NBLK), jnp.int32),
            pltpu.VMEM((SPAN, 512), F32),
            pltpu.VMEM((SPAN, 512), F32),
            pltpu.VMEM((8, 128), jnp.int32),
            pltpu.VMEM((8, 128), jnp.int32),
            pltpu.VMEM((3, NBLK, 128), F32),
            pltpu.VMEM((32, 128), F32),
            pltpu.VMEM((NROW, 8, 128), F32),
            pltpu.VMEM((NROW, 8, 128), F32),
            pltpu.VMEM((SPAN, LINE, 128), F32),
            pltpu.VMEM((NX, LINE, 128), F32),
            pltpu.VMEM((LINE, 128), F32),
            pltpu.VMEM((NY, LINE, 128), F32),
            pltpu.VMEM((ROWS, LINE, 128), F32),
            pltpu.VMEM((1, 128), F32),
            pltpu.VMEM((NROW, 1, 128), F32),
            pltpu.VMEM((2, 24, 128), F32),
            pltpu.VMEM((5, 8, 128), F32),
            pltpu.VMEM((5, 8, 128), F32),
            pltpu.VMEM((24, 128), F32),
            pltpu.VMEM((24, 128), F32),
            pltpu.VMEM((SPAN, 8, 128), F32),
            pltpu.VMEM((SPAN, 8, 128), F32),
            pltpu.VMEM((2, 2, 8, 128), F32),
            pltpu.VMEM((2, 2, 8, 128), F32),
            pltpu.VMEM((HALO + 1, SPAN, 16, 128), F32),
            pltpu.VMEM((HALO + 1, 3, SPAN, 512), F32),
            pltpu.SemaphoreType.REGULAR((4,)),
            dma((8,)),
            dma((7,)),
            dma((7,)),
            dma((12,)),
            dma((12,)),
            dma((4,)),
            dma((4,)),
        ],
        compiler_params=pltpu.CompilerParams(
            collective_id=0, has_side_effects=True, vmem_limit_bytes=16 * 1024 * 1024
        ),
        cost_estimate=pl.CostEstimate(flops=20_000_000, bytes_accessed=600_000, transcendentals=0),
        name="coupling_step",
    )(*[pltpu.with_memory_space_constraint(array, pltpu.HBM) for array in arrays])
    fluid_next, displacement, residual = pl.pallas_call(
        write_out,
        out_shape=shapes,
        in_specs=[vmem] * 3,
        out_specs=(far, far, far),
        scratch_shapes=[dma((3,))],
        compiler_params=pltpu.CompilerParams(vmem_limit_bytes=1024 * 1024),
        name="write_out",
    )(*[pltpu.with_memory_space_constraint(result, pltpu.VMEM) for result in results])
    return fluid_next.reshape(5, 4, 8, 128), displacement, residual


def solution(mesh):
    return jax.shard_map(
        per_device,
        mesh=mesh,
        in_specs=(
            P(None, "brick", "row", None),
            P(("brick", "row"), None),
            P(None, ("brick", "row"), None),
            P(("brick", "row"), None, None),
            P(("brick", "row"), None),
            P(("brick", "row")),
            P("row", None),
            P("row", None),
        ),
        out_specs=(P(None, "brick", "row", None), P(None, "row", None), P(None, "row", None)),
        check_vma=False,
    )
```

```python
import jax
import jax.numpy as jnp
from jax import lax
from jax.experimental import pallas as pl
from jax.experimental.pallas import tpu as pltpu
from jax.sharding import PartitionSpec as P

NX = 8
NY = 8
NBRICK = NX * NY
NROW = 16
NBLK = 16
BP = 64
SPAN = 8
HALO = 3
ROWS = SPAN + 2 * HALO
LINE = 12
FAR_FIRST = (4, 3, 5, 2, 6, 1, 7)
ROW_FAR_FIRST = (8, 7, 9, 6, 10, 5, 11, 4, 12, 3, 13, 2, 14, 1, 15)
CENTRE = 4.0
WIDTH = 4.0
PRESSURE = 0.4
FLUX = 0.05
SMOOTH = 0.1
MESH = pl.DeviceIdType.MESH
F32 = jnp.float32
BF16 = jnp.bfloat16


def iota(shape, axis):
    return lax.broadcasted_iota(jnp.int32, shape, axis)


def select_rows(chosen, values):
    first = values.astype(BF16)
    second = (values - first.astype(F32)).astype(BF16)
    terms = jnp.concatenate([first, second], axis=1)
    both = jnp.dot(chosen.astype(F32).astype(BF16), terms, preferred_element_type=F32)
    return both[:, 0:128] + both[:, 128:256]


def take_lanes(values, index):
    return jnp.take_along_axis(values, index, axis=1, mode="promise_in_bounds")


def sample_pressure(flow, cell, packed_cell, pressure):
    density = flow[0:32, :]
    inverse = 1.0 / density
    kinetic = jnp.zeros_like(density)
    for c in range(3):
        momentum = flow[32 * (c + 1) : 32 * (c + 2), :]
        kinetic = kinetic + momentum * (momentum * inverse)
    pressure[...] = PRESSURE * (flow[128:160, :] - 0.5 * kinetic)
    packed_cell[:, 0:BP] = cell[0:8, :]
    packed_cell[:, BP:128] = cell[8:16, :]
    index = packed_cell[...]
    high = index >> 7
    low = index & 127
    sampled = jnp.zeros((8, 128), F32)
    for k in range(32):
        line = jnp.broadcast_to(pressure[k : k + 1, :], (8, 128))
        sampled = jnp.where(high == k, take_lanes(line, low), sampled)
    swapped = pltpu.roll(sampled, BP, 1)
    left = iota((8, 128), 1) < BP
    return jnp.concatenate(
        [jnp.where(left, sampled, swapped), jnp.where(left, swapped, sampled)], axis=0
    )


def sort_blocks(owner, start, line_of):
    line_of[0:1, :] = jnp.full((1, 128), -1, jnp.int32)
    line_of[1:2, :] = jnp.zeros((1, 128), jnp.int32)
    line_of[0:1, 0:NBLK] = owner[...]
    line_of[1:2, 0:NBLK] = start[...]
    lane = iota((16, 128), 1).astype(F32)
    named = jnp.broadcast_to(line_of[0:1, :], (16, 128))
    mine = named == iota((16, 128), 0)
    first = jnp.min(jnp.where(mine, lane, 999.0), axis=1, keepdims=True)
    is_first = jnp.sum(jnp.where(mine & (lane == first), 1.0, 0.0), axis=0, keepdims=True)
    key = 2.0 * named[0:1, :].astype(F32) + (1.0 - is_first)
    key = jnp.broadcast_to(key, (128, 128))
    begins = jnp.broadcast_to(line_of[1:2, :].astype(F32), (128, 128))
    row = iota((128, 128), 0)
    wanted = (2 * (row >> 3) + (row & 1)).astype(F32)
    begin = jnp.sum(jnp.where(key == wanted, begins, 0.0), axis=1, keepdims=True)
    key = jnp.where(iota((128, 128), 1) < NBLK, key, -1.0)
    again = jnp.maximum(key, jnp.maximum(shifted(key, 16), shifted(key, 32)))
    component = iota((128, 128), 1) >> 4
    chosen = (again == wanted) & (component == ((row & 7) >> 1))
    return chosen[:, 0:48], jnp.broadcast_to(begin, (128, 128))


def shifted(value, by):
    return jnp.broadcast_to(pltpu.roll(value[0:8], by, 1)[0:1], value.shape)


def pack_windows(sampled, normals, doubled, weights, chosen, begin, send):
    doubled[:, :, 0:BP] = normals[...]
    doubled[:, :, BP:128] = normals[...]
    traction = jnp.concatenate([sampled * doubled[c] for c in range(3)], axis=0)
    block = iota((48, 128), 0) & 15
    half = iota((48, 128), 1) >> 6
    spread = [jnp.where(block == 2 * g + half, traction, 0.0).astype(BF16) for g in range(8)]
    forces = jnp.dot(jnp.concatenate(spread, axis=1), weights[...], preferred_element_type=F32)
    windows = select_rows(chosen, forces)
    index = (iota((128, 128), 1) - (begin.astype(jnp.int32) & 127)) & 127
    sub = iota((8, 128), 0)
    for o in range(NROW):
        part = slice(8 * o, 8 * o + 8)
        turned = take_lanes(windows[part], index[part])
        send[o] = jnp.where(sub < 6, turned, begin[part])


def add_windows(received, dense):
    values = received[...].reshape(128, 128)
    low = jnp.broadcast_to(received[:, 6:7, :], (16, 8, 128)).reshape(128, 128)
    high = jnp.broadcast_to(received[:, 7:8, :], (16, 8, 128)).reshape(128, 128)
    row = iota((128, 128), 0)
    lane = iota((128, 128), 1)
    begin = jnp.where((row & 1) == 0, low, high)
    shift = begin.astype(jnp.int32) & 127
    upright = jnp.sum(jnp.where(row == lane, begin, 0.0), axis=0, keepdims=True)
    line = jnp.broadcast_to(upright.astype(jnp.int32) >> 7, (128, 128))
    component = (lane & 7) >> 1
    fits = (component == ((row >> 2) & 3)) & (component < 3)
    place = 4 * (row >> 4) + (row & 3)
    window = (row & 7) < 6
    here = jnp.where(window & (lane >= shift), values, 0.0)
    after = jnp.where(window & (lane < shift), values, 0.0)
    chosen = jnp.concatenate([fits & (place == line), fits & (place == line + 1)], axis=1)
    total = select_rows(chosen, jnp.concatenate([here, after], axis=0))
    for s in range(SPAN):
        dense[s] = total[16 * s : 16 * s + LINE]


def turn(value, by, axis):
    size = value.shape[axis]
    return pltpu.roll(value, by % size, axis)


def next_node(value):
    turned = turn(value, -1, 1)
    sub = iota((8, 128), 0) & 3
    ahead = jnp.where(sub == 3, turn(turned, 3, 0), turn(turned, -1, 0))
    return jnp.where(iota((8, 128), 1) == 127, ahead, turned)


def node_before(value):
    turned = turn(value, 1, 1)
    sub = iota((8, 128), 0) & 3
    behind = jnp.where(sub == 0, turn(turned, -3, 0), turn(turned, 1, 0))
    return jnp.where(iota((8, 128), 1) == 0, behind, turned)


def pieces_along(state, direction):
    density, energy = state[0], state[4]
    inverse = 1.0 / density
    velocity = [state[1 + c] * inverse for c in range(3)]
    kinetic = state[1] * velocity[0] + state[2] * velocity[1] + state[3] * velocity[2]
    pressure = PRESSURE * (energy - 0.5 * kinetic)
    moving = velocity[direction]
    flux = [state[1 + direction]]
    for c in range(3):
        term = state[1 + c] * moving
        flux.append(term + pressure if c == direction else term)
    flux.append((energy + pressure) * moving)
    ahead = [SMOOTH * s + FLUX * f for s, f in zip(state, flux)]
    behind = [SMOOTH * s - FLUX * f for s, f in zip(state, flux)]
    return ahead, behind


def fluid_step(flow, x_low, x_high, y_low, y_high, result):
    own = [[flow[32 * f + 8 * i : 32 * f + 8 * i + 8, :] for f in range(5)] for i in range(4)]
    total = [[(1.0 - 6.0 * SMOOTH) * own[i][f] for f in range(5)] for i in range(4)]
    slab = [[x_low[f] for f in range(5)]] + own + [[x_high[f] for f in range(5)]]
    for i in range(6):
        ahead, behind = pieces_along(slab[i], 0)
        for f in range(5):
            if i <= 3:
                total[i][f] = total[i][f] + ahead[f]
            if i >= 2:
                total[i - 2][f] = total[i - 2][f] + behind[f]
    from_low, _ = pieces_along([y_low[4 * f : 4 * f + 4, :] for f in range(5)], 1)
    _, from_high = pieces_along([y_high[4 * f : 4 * f + 4, :] for f in range(5)], 1)
    sub = iota((8, 128), 0)
    for i in range(4):
        ahead, behind = pieces_along(own[i], 1)
        for f in range(5):
            low = jnp.broadcast_to(from_low[f][i : i + 1, :], (8, 128))
            high = jnp.broadcast_to(from_high[f][i : i + 1, :], (8, 128))
            total[i][f] = total[i][f] + jnp.where(sub == 0, low, turn(ahead[f], 1, 0))
            total[i][f] = total[i][f] + jnp.where(sub == 7, high, turn(behind[f], -1, 0))
        ahead, behind = pieces_along(own[i], 2)
        for f in range(5):
            total[i][f] = total[i][f] + turn(ahead[f], 1, 1) + turn(behind[f], -1, 1)
            result[32 * f + 8 * i : 32 * f + 8 * i + 8, :] = total[i][f]


def lay_stiffness(source, target):
    for s in range(SPAN):
        for j in range(4):
            line = source[s : s + 1, 128 * j : 128 * j + 128]
            target[s, j : j + 1, :] = line
            target[s, 4 + j : 5 + j, :] = line


def kernel(
    flow_far, cell_far, normals_far, weights_far, owner_far, start_far, diag_far, chord_far,
    fluid_next, displacement, residual,
    flow, cell, normals, weights, owner, start, stiff_diag, stiff_chord,
    packed_cell, line_of, doubled, pressure, windows_out, windows_in, dense, x_in, x_sum, y_in, lines,
    shares_out, shares_in, y_edges, x_low, x_high, y_low, y_high,
    diag_rows, chord_rows, diag_halo, chord_halo, factors, fields, turned,
    reach, load_sem, send_sem, recv_sem, fluid_send, fluid_recv, stiff_send, stiff_recv,
):
    brick = lax.axis_index("brick")
    row = lax.axis_index("row")
    x = lax.div(brick, NY)
    y = lax.rem(brick, NY)
    row_up = lax.rem(row + 1, NROW)
    row_down = lax.rem(row + NROW - 1, NROW)
    brick_up = lax.rem(brick + 1, NBRICK)
    brick_down = lax.rem(brick + NBRICK - 1, NBRICK)

    def x_peer(k):
        return lax.rem(x + k, NX) * NY + y

    def y_peer(k):
        return x * NY + lax.rem(y + k, NY)

    barrier = pltpu.get_barrier_semaphore()

    def greet(to_brick, to_row):
        pl.semaphore_signal(barrier, inc=1, device_id=(to_brick, to_row), device_id_type=MESH)

    for k in ROW_FAR_FIRST:
        greet(brick, lax.rem(row + k, NROW))

    loads = [
        pltpu.make_async_copy(far, near, load_sem.at[n])
        for n, (far, near) in enumerate((
            (flow_far, flow), (cell_far, cell), (weights_far, weights), (normals_far, normals),
            (owner_far, owner), (start_far, start), (diag_far, stiff_diag), (chord_far, stiff_chord),
        ))
    ]
    for load in loads:
        load.start()

    near = ((x_peer(1), row), (x_peer(NX - 1), row), (y_peer(1), row), (y_peer(NY - 1), row))
    for to in near + ((brick_up, row), (brick_down, row)):
        greet(*to)

    def copy_to(source, target, send, receive, to_brick, to_row):
        return pltpu.make_async_remote_copy(
            src_ref=source, dst_ref=target, send_sem=send, recv_sem=receive,
            device_id=(to_brick, to_row), device_id_type=MESH,
        )

    loads[4].wait()
    loads[5].wait()
    chosen, begin = sort_blocks(owner, start, line_of)
    loads[0].wait()
    loads[1].wait()
    sampled = sample_pressure(flow, cell, packed_cell, pressure)
    loads[2].wait()
    loads[3].wait()
    pack_windows(sampled, normals, doubled, weights, chosen, begin, windows_out)
    y_edges[...] = jnp.zeros((2, 24, 128), F32)
    y_edges[0, 0:20, :] = flow[pl.ds(0, 20, stride=8), :]
    y_edges[1, 0:20, :] = flow[pl.ds(7, 20, stride=8), :]

    pl.semaphore_wait(barrier, (NROW - 1) + 6)

    def tell(semaphore, to):
        pl.semaphore_signal(semaphore, inc=1, device_id=to, device_id_type=MESH)

    for n, to in enumerate(near):
        tell(reach.at[n // 2], to)

    for k in ROW_FAR_FIRST:
        to = lax.rem(row + k, NROW)
        copy_to(windows_out.at[to], windows_in.at[row], send_sem.at[0], recv_sem.at[0], brick, to).start()

    windows_in[row] = windows_out[row]

    for axis in range(2):
        pl.semaphore_wait(reach.at[axis], 2)
    for n, to in enumerate(((x_peer(2), row), (x_peer(NX - 2), row), (y_peer(2), row), (y_peer(NY - 2), row))):
        tell(reach.at[2 + n // 2], to)

    fluid_copies = [
        copy_to(y_edges.at[0], y_high, fluid_send.at[0], fluid_recv.at[0], brick, row_down),
        copy_to(y_edges.at[1], y_low, fluid_send.at[1], fluid_recv.at[1], brick, row_up),
    ]
    for f in range(5):
        plane = flow.at[pl.ds(32 * f, 8)]
        fluid_copies.append(
            copy_to(plane, x_high.at[f], fluid_send.at[2 + f], fluid_recv.at[2 + f], brick_down, row)
        )
        plane = flow.at[pl.ds(32 * f + 24, 8)]
        fluid_copies.append(
            copy_to(plane, x_low.at[f], fluid_send.at[7 + f], fluid_recv.at[7 + f], brick_up, row)
        )
    for copy in fluid_copies:
        copy.start()
    loads[6].wait()
    loads[7].wait()
    lay_stiffness(stiff_diag, diag_rows)
    lay_stiffness(stiff_chord, chord_rows)
    stiff_copies = []
    for n, (rows, halo) in enumerate(((diag_rows, diag_halo), (chord_rows, chord_halo))):
        stiff_copies.append(
            copy_to(rows.at[pl.ds(SPAN - 2, 2)], halo.at[0], stiff_send.at[2 * n], stiff_recv.at[2 * n], brick, row_up)
        )
        stiff_copies.append(
            copy_to(rows.at[pl.ds(0, 2)], halo.at[1], stiff_send.at[2 * n + 1], stiff_recv.at[2 * n + 1], brick, row_down)
        )
    for copy in stiff_copies:
        copy.start()

    def await_copies(buffer, count, n):
        part = buffer.at[pl.ds(0, count)]
        copy_to(part, part, send_sem.at[n], recv_sem.at[n], brick_up, row).wait_recv()

    await_copies(windows_in, NROW - 1, 0)
    add_windows(windows_in, dense)

    pl.semaphore_wait(reach.at[2], 2)

    for k in FAR_FIRST:
        to = lax.rem(x + k, NX)
        copy_to(dense.at[to], x_in.at[x], send_sem.at[1], recv_sem.at[1], x_peer(k), row).start()

    x_in[x] = dense[x]
    await_copies(x_in, NX - 1, 1)
    total = x_in[0]
    for k in range(1, NX):
        total = total + x_in[k]
    x_sum[...] = total

    pl.semaphore_wait(reach.at[3], 2)

    for k in FAR_FIRST:
        copy_to(x_sum, y_in.at[y], send_sem.at[2], recv_sem.at[2], y_peer(k), row).start()

    y_in[y] = total

    for copy in fluid_copies:
        copy.wait_recv()
    fluid_step(flow, x_low, x_high, y_low, y_high, fluid_next)
    for copy in stiff_copies:
        copy.wait_recv()
    for i in range(1, ROWS - 1):
        if i < HALO:
            own_diag, own_chord = diag_halo[0, i - 1], chord_halo[0, i - 1]
        elif i < HALO + SPAN:
            own_diag, own_chord = diag_rows[i - HALO], chord_rows[i - HALO]
        else:
            own_diag, own_chord = diag_halo[1, i - HALO - SPAN], chord_halo[1, i - HALO - SPAN]
        chord_before = node_before(own_chord)
        factors[0, i] = (own_diag + (2.0 - CENTRE) + (own_chord + chord_before)) * (1.0 / WIDTH)
        factors[1, i] = own_chord * (1.0 / WIDTH)
        factors[2, i] = chord_before * (1.0 / WIDTH)

    await_copies(y_in, NY - 1, 2)
    total = y_in[0]
    for k in range(1, NY):
        total = total + y_in[k]
    lines[HALO + x] = total

    own_line = lines.at[HALO + x]

    goes_up = (x >= SPAN - HALO) & (row < NROW - 1)
    goes_down = (x < HALO) & (row > 0)

    def send_beside(steps):
        @pl.when(goes_up)
        def _():
            for k in steps:
                target = lines.at[x - (SPAN - HALO)]
                copy_to(own_line, target, send_sem.at[4], recv_sem.at[4], x_peer(k), row_up).start()

        @pl.when(goes_down)
        def _():
            for k in steps:
                target = lines.at[HALO + SPAN + x]
                copy_to(own_line, target, send_sem.at[5], recv_sem.at[5], x_peer(k), row_down).start()

    send_beside((4, 3, 5))
    for k in FAR_FIRST:
        copy_to(own_line, own_line, send_sem.at[3], recv_sem.at[3], x_peer(k), row).start()
    send_beside((2, 6, 1, 7, 0))

    @pl.when(row == 0)
    def _():
        lines[0:HALO] = jnp.zeros((HALO, LINE, 128), F32)

    @pl.when(row == NROW - 1)
    def _():
        lines[HALO + SPAN : ROWS] = jnp.zeros((HALO, LINE, 128), F32)

    await_copies(lines, NX - 1, 3)

    @pl.when(row > 0)
    def _():
        await_copies(lines, HALO, 4)

    @pl.when(row < NROW - 1)
    def _():
        await_copies(lines, HALO, 5)

    below = jnp.where(row > 0, 1.0, 0.0).astype(F32)
    above = jnp.where(row < NROW - 1, 1.0, 0.0).astype(F32)
    products = [jnp.zeros((8, 128), F32) for _ in range(6)]
    for half in range(2):
        part = slice(8 * half, 8 * half + 8)
        if half == 0:
            levels = [[lines[i, 0:8, :] for i in range(ROWS)]]
        else:
            spare = jnp.zeros((4, 128), F32)
            levels = [[jnp.concatenate([lines[i, 8:LINE, :], spare], axis=0) for i in range(ROWS)]]
        for level in range(1, HALO + 1):
            before = levels[-1]
            after = [None] * ROWS
            for i in range(level, ROWS - level):
                sides = (1.0 / WIDTH) * (before[i - 1] + before[i + 1])
                around = factors[1, i] * next_node(before[i]) + factors[2, i] * node_before(before[i])
                value = factors[0, i] * before[i] - sides - around
                if i < HALO:
                    value = value * below
                if i >= HALO + SPAN:
                    value = value * above
                after[i] = value
            levels.append(after)
        for i in range(HALO, HALO + SPAN):
            for level in range(HALO + 1):
                fields[level, i - HALO, part, :] = levels[level][i]
            for n, (p, q) in enumerate(((0, 0), (0, 1), (1, 1), (1, 2), (2, 2), (2, 3))):
                products[n] = products[n] + levels[p][i] * levels[q][i]
    share = jnp.zeros((1, 128), F32)
    lane = iota((1, 128), 1)
    for n in range(6):
        inner = jnp.sum(jnp.sum(products[n], axis=0, keepdims=True), axis=1, keepdims=True)
        share = jnp.where(lane == n, jnp.broadcast_to(inner, (1, 128)), share)
    shares_out[...] = share

    for k in ROW_FAR_FIRST:
        to = lax.rem(row + k, NROW)
        copy_to(shares_out, shares_in.at[row], send_sem.at[6], recv_sem.at[6], brick, to).start()

    shares_in[row] = shares_out[...]

    for level in range(HALO + 1):
        for s in range(SPAN):
            for c in range(3):
                for j in range(4):
                    line = fields[level, s, 4 * c + j : 4 * c + j + 1, :]
                    turned[level, c, s : s + 1, 128 * j : 128 * j + 128] = line

    await_copies(shares_in, NROW - 1, 6)
    share = shares_in[0]
    for k in range(1, NROW):
        share = share + shares_in[k]
    moment = [jnp.broadcast_to(share[:, n : n + 1], (8, 128)) for n in range(6)]
    matrix = [CENTRE * moment[n] + WIDTH * moment[n + 1] for n in range(5)]
    m00, m01, m02, m11, m12, m22 = matrix[0], matrix[1], matrix[2], matrix[2], matrix[3], matrix[4]
    l10 = m01 / m00
    l20 = m02 / m00
    d1 = m11 - l10 * m01
    e = m12 - l10 * m02
    l21 = e / d1
    d2 = m22 - l20 * m02 - l21 * e
    y1 = moment[1] - l10 * moment[0]
    y2 = moment[2] - l20 * moment[0] - l21 * y1
    w2 = y2 / d2
    w1 = y1 / d1 - l21 * w2
    w0 = moment[0] / m00 - l10 * w1 - l20 * w2
    r0 = 1.0 - CENTRE * w0
    r1 = -(WIDTH * w0 + CENTRE * w1)
    r2 = -(WIDTH * w1 + CENTRE * w2)
    r3 = -(WIDTH * w2)
    for c in range(3):
        for j in range(4):
            part = slice(128 * j, 128 * j + 128)
            v = [turned[level, c, :, part] for level in range(4)]
            displacement[c, :, part] = w0 * v[0] + w1 * v[1] + w2 * v[2]
            residual[c, :, part] = (r0 * v[0] + r1 * v[1]) + (r2 * v[2] + r3 * v[3])

    def await_sent(buffer, count, n):
        part = buffer.at[pl.ds(0, count)]
        copy_to(part, part, send_sem.at[n], recv_sem.at[n], brick_up, row).wait_send()

    await_sent(windows_in, NROW - 1, 0)
    await_sent(x_in, NX - 1, 1)
    await_sent(y_in, NY - 1, 2)
    await_sent(lines, NX - 1, 3)

    @pl.when(goes_up)
    def _():
        await_sent(lines, NX, 4)

    @pl.when(goes_down)
    def _():
        await_sent(lines, NX, 5)

    await_sent(shares_in, NROW - 1, 6)
    for copy in fluid_copies + stiff_copies:
        copy.wait_send()


def write_out(fluid, displacement, residual, fluid_far, displacement_far, residual_far, sem):
    copies = [
        pltpu.make_async_copy(near, far, sem.at[n])
        for n, (near, far) in enumerate(
            ((fluid, fluid_far), (displacement, displacement_far), (residual, residual_far))
        )
    ]
    for copy in copies:
        copy.start()
    for copy in copies:
        copy.wait()


def per_device(
    flow_state, point_cell, normals, rbf_weights, block_owner, block_start, stiff_diag, stiff_chord
):
    flow = flow_state.reshape(160, 128)
    weights = rbf_weights.reshape(NBLK * BP, 128)
    owner = block_owner.reshape(1, NBLK)
    start = block_start.reshape(1, NBLK)
    arrays = (flow, point_cell, normals, weights, owner, start, stiff_diag, stiff_chord)
    vmem = pl.BlockSpec(memory_space=pltpu.VMEM)
    far = pl.BlockSpec(memory_space=pltpu.HBM)
    dma = pltpu.SemaphoreType.DMA
    shapes = (
        jax.ShapeDtypeStruct((160, 128), F32),
        jax.ShapeDtypeStruct((3, SPAN, 512), F32),
        jax.ShapeDtypeStruct((3, SPAN, 512), F32),
    )
    results = pl.pallas_call(
        kernel,
        out_shape=shapes,
        in_specs=[far] * 8,
        out_specs=(vmem, vmem, vmem),
        scratch_shapes=[
            pltpu.VMEM((160, 128), F32),
            pltpu.VMEM((NBLK, BP), jnp.int32),
            pltpu.VMEM((3, NBLK, BP), F32),
            pltpu.VMEM((NBLK * BP, 128), BF16),
            pltpu.VMEM((1, NBLK), jnp.int32),
            pltpu.VMEM((1, NBLK), jnp.int32),
            pltpu.VMEM((SPAN, 512), F32),
            pltpu.VMEM((SPAN, 512), F32),
            pltpu.VMEM((8, 128), jnp.int32),
            pltpu.VMEM((8, 128), jnp.int32),
            pltpu.VMEM((3, NBLK, 128), F32),
            pltpu.VMEM((32, 128), F32),
            pltpu.VMEM((NROW, 8, 128), F32),
            pltpu.VMEM((NROW, 8, 128), F32),
            pltpu.VMEM((SPAN, LINE, 128), F32),
            pltpu.VMEM((NX, LINE, 128), F32),
            pltpu.VMEM((LINE, 128), F32),
            pltpu.VMEM((NY, LINE, 128), F32),
            pltpu.VMEM((ROWS, LINE, 128), F32),
            pltpu.VMEM((1, 128), F32),
            pltpu.VMEM((NROW, 1, 128), F32),
            pltpu.VMEM((2, 24, 128), F32),
            pltpu.VMEM((5, 8, 128), F32),
            pltpu.VMEM((5, 8, 128), F32),
            pltpu.VMEM((24, 128), F32),
            pltpu.VMEM((24, 128), F32),
            pltpu.VMEM((SPAN, 8, 128), F32),
            pltpu.VMEM((SPAN, 8, 128), F32),
            pltpu.VMEM((2, 2, 8, 128), F32),
            pltpu.VMEM((2, 2, 8, 128), F32),
            pltpu.VMEM((3, ROWS, 8, 128), F32),
            pltpu.VMEM((HALO + 1, SPAN, 16, 128), F32),
            pltpu.VMEM((HALO + 1, 3, SPAN, 512), F32),
            pltpu.SemaphoreType.REGULAR((4,)),
            dma((8,)),
            dma((7,)),
            dma((7,)),
            dma((12,)),
            dma((12,)),
            dma((4,)),
            dma((4,)),
        ],
        compiler_params=pltpu.CompilerParams(
            collective_id=0, has_side_effects=True, vmem_limit_bytes=16 * 1024 * 1024
        ),
        cost_estimate=pl.CostEstimate(flops=20_000_000, bytes_accessed=600_000, transcendentals=0),
        name="coupling_step",
    )(*[pltpu.with_memory_space_constraint(array, pltpu.HBM) for array in arrays])
    fluid_next, displacement, residual = pl.pallas_call(
        write_out,
        out_shape=shapes,
        in_specs=[vmem] * 3,
        out_specs=(far, far, far),
        scratch_shapes=[dma((3,))],
        compiler_params=pltpu.CompilerParams(vmem_limit_bytes=1024 * 1024),
        name="write_out",
    )(*[pltpu.with_memory_space_constraint(result, pltpu.VMEM) for result in results])
    return fluid_next.reshape(5, 4, 8, 128), displacement, residual


def solution(mesh):
    return jax.shard_map(
        per_device,
        mesh=mesh,
        in_specs=(
            P(None, "brick", "row", None),
            P(("brick", "row"), None),
            P(None, ("brick", "row"), None),
            P(("brick", "row"), None, None),
            P(("brick", "row"), None),
            P(("brick", "row")),
            P("row", None),
            P("row", None),
        ),
        out_specs=(P(None, "brick", "row", None), P(None, "row", None), P(None, "row", None)),
        check_vma=False,
    )
```

```python
import jax
import jax.numpy as jnp
from jax import lax
from jax.experimental import pallas as pl
from jax.experimental.pallas import tpu as pltpu
from jax.sharding import PartitionSpec as P

NX = 8
NY = 8
NBRICK = NX * NY
NROW = 16
NBLK = 16
BP = 64
SPAN = 8
HALO = 3
ROWS = SPAN + 2 * HALO
LINE = 12
FAR_FIRST = (4, 3, 5, 2, 6, 1, 7)
ROW_FAR_FIRST = (8, 7, 9, 6, 10, 5, 11, 4, 12, 3, 13, 2, 14, 1, 15)
CENTRE = 4.0
WIDTH = 4.0
PRESSURE = 0.4
FLUX = 0.05
SMOOTH = 0.1
MESH = pl.DeviceIdType.MESH
F32 = jnp.float32
BF16 = jnp.bfloat16


def iota(shape, axis):
    return lax.broadcasted_iota(jnp.int32, shape, axis)


def select_rows(chosen, values):
    first = values.astype(BF16)
    second = (values - first.astype(F32)).astype(BF16)
    terms = jnp.concatenate([first, second], axis=1)
    both = jnp.dot(chosen.astype(F32).astype(BF16), terms, preferred_element_type=F32)
    return both[:, 0:128] + both[:, 128:256]


def take_lanes(values, index):
    return jnp.take_along_axis(values, index, axis=1, mode="promise_in_bounds")


def sample_pressure(flow, cell, packed_cell, pressure):
    density = flow[0:32, :]
    inverse = 1.0 / density
    kinetic = jnp.zeros_like(density)
    for c in range(3):
        momentum = flow[32 * (c + 1) : 32 * (c + 2), :]
        kinetic = kinetic + momentum * (momentum * inverse)
    pressure[...] = PRESSURE * (flow[128:160, :] - 0.5 * kinetic)
    packed_cell[:, 0:BP] = cell[0:8, :]
    packed_cell[:, BP:128] = cell[8:16, :]
    index = packed_cell[...]
    high = index >> 7
    low = index & 127
    sampled = jnp.zeros((8, 128), F32)
    for k in range(32):
        line = jnp.broadcast_to(pressure[k : k + 1, :], (8, 128))
        sampled = jnp.where(high == k, take_lanes(line, low), sampled)
    swapped = pltpu.roll(sampled, BP, 1)
    left = iota((8, 128), 1) < BP
    return jnp.concatenate(
        [jnp.where(left, sampled, swapped), jnp.where(left, swapped, sampled)], axis=0
    )


def sort_blocks(owner, start, line_of):
    line_of[0:1, :] = jnp.full((1, 128), -1, jnp.int32)
    line_of[1:2, :] = jnp.zeros((1, 128), jnp.int32)
    line_of[0:1, 0:NBLK] = owner[...]
    line_of[1:2, 0:NBLK] = start[...]
    lane = iota((16, 128), 1).astype(F32)
    named = jnp.broadcast_to(line_of[0:1, :], (16, 128))
    mine = named == iota((16, 128), 0)
    first = jnp.min(jnp.where(mine, lane, 999.0), axis=1, keepdims=True)
    is_first = jnp.sum(jnp.where(mine & (lane == first), 1.0, 0.0), axis=0, keepdims=True)
    key = 2.0 * named[0:1, :].astype(F32) + (1.0 - is_first)
    key = jnp.broadcast_to(key, (128, 128))
    begins = jnp.broadcast_to(line_of[1:2, :].astype(F32), (128, 128))
    row = iota((128, 128), 0)
    wanted = (2 * (row >> 3) + (row & 1)).astype(F32)
    begin = jnp.sum(jnp.where(key == wanted, begins, 0.0), axis=1, keepdims=True)
    key = jnp.where(iota((128, 128), 1) < NBLK, key, -1.0)
    again = jnp.maximum(key, jnp.maximum(shifted(key, 16), shifted(key, 32)))
    component = iota((128, 128), 1) >> 4
    chosen = (again == wanted) & (component == ((row & 7) >> 1))
    return chosen[:, 0:48], jnp.broadcast_to(begin, (128, 128))


def shifted(value, by):
    return jnp.broadcast_to(pltpu.roll(value[0:8], by, 1)[0:1], value.shape)


def pack_windows(sampled, normals, doubled, weights, chosen, begin, send):
    doubled[:, :, 0:BP] = normals[...]
    doubled[:, :, BP:128] = normals[...]
    traction = jnp.concatenate([sampled * doubled[c] for c in range(3)], axis=0)
    block = iota((48, 128), 0) & 15
    half = iota((48, 128), 1) >> 6
    spread = [jnp.where(block == 2 * g + half, traction, 0.0).astype(BF16) for g in range(8)]
    forces = jnp.dot(jnp.concatenate(spread, axis=1), weights[...], preferred_element_type=F32)
    windows = select_rows(chosen, forces)
    index = (iota((128, 128), 1) - (begin.astype(jnp.int32) & 127)) & 127
    sub = iota((8, 128), 0)
    for o in range(NROW):
        part = slice(8 * o, 8 * o + 8)
        turned = take_lanes(windows[part], index[part])
        send[o] = jnp.where(sub < 6, turned, begin[part])


def add_windows(received, dense):
    values = received[...].reshape(128, 128)
    low = jnp.broadcast_to(received[:, 6:7, :], (16, 8, 128)).reshape(128, 128)
    high = jnp.broadcast_to(received[:, 7:8, :], (16, 8, 128)).reshape(128, 128)
    row = iota((128, 128), 0)
    lane = iota((128, 128), 1)
    begin = jnp.where((row & 1) == 0, low, high)
    shift = begin.astype(jnp.int32) & 127
    upright = jnp.sum(jnp.where(row == lane, begin, 0.0), axis=0, keepdims=True)
    line = jnp.broadcast_to(upright.astype(jnp.int32) >> 7, (128, 128))
    component = (lane & 7) >> 1
    fits = (component == ((row >> 2) & 3)) & (component < 3)
    place = 4 * (row >> 4) + (row & 3)
    window = (row & 7) < 6
    here = jnp.where(window & (lane >= shift), values, 0.0)
    after = jnp.where(window & (lane < shift), values, 0.0)
    chosen = jnp.concatenate([fits & (place == line), fits & (place == line + 1)], axis=1)
    total = select_rows(chosen, jnp.concatenate([here, after], axis=0))
    for s in range(SPAN):
        dense[s] = total[16 * s : 16 * s + LINE]


def turn(value, by, axis):
    size = value.shape[axis]
    return pltpu.roll(value, by % size, axis)


def next_node(value):
    turned = turn(value, -1, 1)
    sub = iota((8, 128), 0) & 3
    ahead = jnp.where(sub == 3, turn(turned, 3, 0), turn(turned, -1, 0))
    return jnp.where(iota((8, 128), 1) == 127, ahead, turned)


def node_before(value):
    turned = turn(value, 1, 1)
    sub = iota((8, 128), 0) & 3
    behind = jnp.where(sub == 0, turn(turned, -3, 0), turn(turned, 1, 0))
    return jnp.where(iota((8, 128), 1) == 0, behind, turned)


def pieces_along(state, direction):
    density, energy = state[0], state[4]
    inverse = 1.0 / density
    velocity = [state[1 + c] * inverse for c in range(3)]
    kinetic = state[1] * velocity[0] + state[2] * velocity[1] + state[3] * velocity[2]
    pressure = PRESSURE * (energy - 0.5 * kinetic)
    moving = velocity[direction]
    flux = [state[1 + direction]]
    for c in range(3):
        term = state[1 + c] * moving
        flux.append(term + pressure if c == direction else term)
    flux.append((energy + pressure) * moving)
    ahead = [SMOOTH * s + FLUX * f for s, f in zip(state, flux)]
    behind = [SMOOTH * s - FLUX * f for s, f in zip(state, flux)]
    return ahead, behind


def fluid_step(flow, x_low, x_high, y_low, y_high, result):
    own = [[flow[32 * f + 8 * i : 32 * f + 8 * i + 8, :] for f in range(5)] for i in range(4)]
    total = [[(1.0 - 6.0 * SMOOTH) * own[i][f] for f in range(5)] for i in range(4)]
    slab = [[x_low[f] for f in range(5)]] + own + [[x_high[f] for f in range(5)]]
    for i in range(6):
        ahead, behind = pieces_along(slab[i], 0)
        for f in range(5):
            if i <= 3:
                total[i][f] = total[i][f] + ahead[f]
            if i >= 2:
                total[i - 2][f] = total[i - 2][f] + behind[f]
    from_low, _ = pieces_along([y_low[4 * f : 4 * f + 4, :] for f in range(5)], 1)
    _, from_high = pieces_along([y_high[4 * f : 4 * f + 4, :] for f in range(5)], 1)
    sub = iota((8, 128), 0)
    for i in range(4):
        ahead, behind = pieces_along(own[i], 1)
        for f in range(5):
            low = jnp.broadcast_to(from_low[f][i : i + 1, :], (8, 128))
            high = jnp.broadcast_to(from_high[f][i : i + 1, :], (8, 128))
            total[i][f] = total[i][f] + jnp.where(sub == 0, low, turn(ahead[f], 1, 0))
            total[i][f] = total[i][f] + jnp.where(sub == 7, high, turn(behind[f], -1, 0))
        ahead, behind = pieces_along(own[i], 2)
        for f in range(5):
            total[i][f] = total[i][f] + turn(ahead[f], 1, 1) + turn(behind[f], -1, 1)
            result[32 * f + 8 * i : 32 * f + 8 * i + 8, :] = total[i][f]


def lay_stiffness(source, target):
    for s in range(SPAN):
        for j in range(4):
            line = source[s : s + 1, 128 * j : 128 * j + 128]
            target[s, j : j + 1, :] = line
            target[s, 4 + j : 5 + j, :] = line


def kernel(
    flow_far, cell_far, normals_far, weights_far, owner_far, start_far, diag_far, chord_far,
    fluid_next, displacement, residual,
    flow, cell, normals, weights, owner, start, stiff_diag, stiff_chord,
    packed_cell, line_of, doubled, pressure, windows_out, windows_in, dense, x_in, x_sum, y_in, lines,
    shares_out, shares_in, y_edges, x_low, x_high, y_low, y_high,
    diag_rows, chord_rows, diag_halo, chord_halo, factors, fields, turned,
    reach, load_sem, send_sem, recv_sem, fluid_send, fluid_recv, stiff_send, stiff_recv,
):
    brick = lax.axis_index("brick")
    row = lax.axis_index("row")
    x = lax.div(brick, NY)
    y = lax.rem(brick, NY)
    row_up = lax.rem(row + 1, NROW)
    row_down = lax.rem(row + NROW - 1, NROW)
    brick_up = lax.rem(brick + 1, NBRICK)
    brick_down = lax.rem(brick + NBRICK - 1, NBRICK)

    def x_peer(k):
        return lax.rem(x + k, NX) * NY + y

    def y_peer(k):
        return x * NY + lax.rem(y + k, NY)

    barrier = pltpu.get_barrier_semaphore()

    def greet(to_brick, to_row):
        pl.semaphore_signal(barrier, inc=1, device_id=(to_brick, to_row), device_id_type=MESH)

    for k in ROW_FAR_FIRST:
        greet(brick, lax.rem(row + k, NROW))

    loads = [
        pltpu.make_async_copy(far, near, load_sem.at[n])
        for n, (far, near) in enumerate((
            (flow_far, flow), (cell_far, cell), (weights_far, weights), (normals_far, normals),
            (owner_far, owner), (start_far, start), (diag_far, stiff_diag), (chord_far, stiff_chord),
        ))
    ]
    for load in loads:
        load.start()

    near = ((x_peer(1), row), (x_peer(NX - 1), row), (y_peer(1), row), (y_peer(NY - 1), row))
    for to in near + ((brick_up, row), (brick_down, row)):
        greet(*to)

    def copy_to(source, target, send, receive, to_brick, to_row):
        return pltpu.make_async_remote_copy(
            src_ref=source, dst_ref=target, send_sem=send, recv_sem=receive,
            device_id=(to_brick, to_row), device_id_type=MESH,
        )

    loads[4].wait()
    loads[5].wait()
    chosen, begin = sort_blocks(owner, start, line_of)
    loads[0].wait()
    loads[1].wait()
    sampled = sample_pressure(flow, cell, packed_cell, pressure)
    loads[2].wait()
    loads[3].wait()
    pack_windows(sampled, normals, doubled, weights, chosen, begin, windows_out)
    y_edges[...] = jnp.zeros((2, 24, 128), F32)
    y_edges[0, 0:20, :] = flow[pl.ds(0, 20, stride=8), :]
    y_edges[1, 0:20, :] = flow[pl.ds(7, 20, stride=8), :]

    pl.semaphore_wait(barrier, (NROW - 1) + 6)

    def tell(semaphore, to):
        pl.semaphore_signal(semaphore, inc=1, device_id=to, device_id_type=MESH)

    for n, to in enumerate(near):
        tell(reach.at[n // 2], to)

    for k in ROW_FAR_FIRST:
        to = lax.rem(row + k, NROW)
        copy_to(windows_out.at[to], windows_in.at[row], send_sem.at[0], recv_sem.at[0], brick, to).start()

    windows_in[row] = windows_out[row]

    for axis in range(2):
        pl.semaphore_wait(reach.at[axis], 2)
    for n, to in enumerate(((x_peer(2), row), (x_peer(NX - 2), row), (y_peer(2), row), (y_peer(NY - 2), row))):
        tell(reach.at[2 + n // 2], to)

    fluid_copies = [
        copy_to(y_edges.at[0], y_high, fluid_send.at[0], fluid_recv.at[0], brick, row_down),
        copy_to(y_edges.at[1], y_low, fluid_send.at[1], fluid_recv.at[1], brick, row_up),
    ]
    for f in range(5):
        plane = flow.at[pl.ds(32 * f, 8)]
        fluid_copies.append(
            copy_to(plane, x_high.at[f], fluid_send.at[2 + f], fluid_recv.at[2 + f], brick_down, row)
        )
        plane = flow.at[pl.ds(32 * f + 24, 8)]
        fluid_copies.append(
            copy_to(plane, x_low.at[f], fluid_send.at[7 + f], fluid_recv.at[7 + f], brick_up, row)
        )
    for copy in fluid_copies:
        copy.start()
    loads[6].wait()
    loads[7].wait()
    lay_stiffness(stiff_diag, diag_rows)
    lay_stiffness(stiff_chord, chord_rows)
    stiff_copies = []
    for n, (rows, halo) in enumerate(((diag_rows, diag_halo), (chord_rows, chord_halo))):
        stiff_copies.append(
            copy_to(rows.at[pl.ds(SPAN - 2, 2)], halo.at[0], stiff_send.at[2 * n], stiff_recv.at[2 * n], brick, row_up)
        )
        stiff_copies.append(
            copy_to(rows.at[pl.ds(0, 2)], halo.at[1], stiff_send.at[2 * n + 1], stiff_recv.at[2 * n + 1], brick, row_down)
        )
    for copy in stiff_copies:
        copy.start()

    def await_copies(buffer, count, n):
        part = buffer.at[pl.ds(0, count)]
        copy_to(part, part, send_sem.at[n], recv_sem.at[n], brick_up, row).wait_recv()

    await_copies(windows_in, NROW - 1, 0)
    add_windows(windows_in, dense)

    pl.semaphore_wait(reach.at[2], 2)

    for k in FAR_FIRST:
        to = lax.rem(x + k, NX)
        copy_to(dense.at[to], x_in.at[x], send_sem.at[1], recv_sem.at[1], x_peer(k), row).start()

    x_in[x] = dense[x]
    await_copies(x_in, NX - 1, 1)
    total = x_in[0]
    for k in range(1, NX):
        total = total + x_in[k]
    x_sum[...] = total

    pl.semaphore_wait(reach.at[3], 2)

    for k in FAR_FIRST:
        copy_to(x_sum, y_in.at[y], send_sem.at[2], recv_sem.at[2], y_peer(k), row).start()

    y_in[y] = total

    for copy in fluid_copies:
        copy.wait_recv()
    fluid_step(flow, x_low, x_high, y_low, y_high, fluid_next)
    for copy in stiff_copies:
        copy.wait_recv()
    for i in range(1, ROWS - 1):
        if i < HALO:
            own_diag, own_chord = diag_halo[0, i - 1], chord_halo[0, i - 1]
        elif i < HALO + SPAN:
            own_diag, own_chord = diag_rows[i - HALO], chord_rows[i - HALO]
        else:
            own_diag, own_chord = diag_halo[1, i - HALO - SPAN], chord_halo[1, i - HALO - SPAN]
        chord_before = node_before(own_chord)
        factors[0, i] = (own_diag + (2.0 - CENTRE) + (own_chord + chord_before)) * (1.0 / WIDTH)
        factors[1, i] = own_chord * (1.0 / WIDTH)
        factors[2, i] = chord_before * (1.0 / WIDTH)

    await_copies(y_in, NY - 1, 2)
    total = y_in[0]
    for k in range(1, NY):
        total = total + y_in[k]
    lines[HALO + x] = total

    own_line = lines.at[HALO + x]

    goes_up = (x >= SPAN - HALO) & (row < NROW - 1)
    goes_down = (x < HALO) & (row > 0)

    def send_beside(steps):
        @pl.when(goes_up)
        def _():
            for k in steps:
                target = lines.at[x - (SPAN - HALO)]
                copy_to(own_line, target, send_sem.at[4], recv_sem.at[4], x_peer(k), row_up).start()

        @pl.when(goes_down)
        def _():
            for k in steps:
                target = lines.at[HALO + SPAN + x]
                copy_to(own_line, target, send_sem.at[5], recv_sem.at[5], x_peer(k), row_down).start()

    send_beside((4, 3, 5))
    for k in FAR_FIRST:
        copy_to(own_line, own_line, send_sem.at[3], recv_sem.at[3], x_peer(k), row).start()
    send_beside((2, 6, 1, 7, 0))

    @pl.when(row == 0)
    def _():
        lines[0:HALO] = jnp.zeros((HALO, LINE, 128), F32)

    @pl.when(row == NROW - 1)
    def _():
        lines[HALO + SPAN : ROWS] = jnp.zeros((HALO, LINE, 128), F32)

    await_copies(lines, NX - 1, 3)

    @pl.when(row > 0)
    def _():
        await_copies(lines, HALO, 4)

    @pl.when(row < NROW - 1)
    def _():
        await_copies(lines, HALO, 5)

    below = jnp.where(row > 0, 1.0, 0.0).astype(F32)
    above = jnp.where(row < NROW - 1, 1.0, 0.0).astype(F32)
    products = [jnp.zeros((8, 128), F32) for _ in range(6)]
    kept = []
    for half in range(2):
        part = slice(8 * half, 8 * half + 8)
        if half == 0:
            levels = [[lines[i, 0:8, :] for i in range(ROWS)]]
        else:
            spare = jnp.zeros((4, 128), F32)
            levels = [[jnp.concatenate([lines[i, 8:LINE, :], spare], axis=0) for i in range(ROWS)]]
        for level in range(1, HALO + 1):
            before = levels[-1]
            after = [None] * ROWS
            for i in range(level, ROWS - level):
                sides = (1.0 / WIDTH) * (before[i - 1] + before[i + 1])
                around = factors[1, i] * next_node(before[i]) + factors[2, i] * node_before(before[i])
                value = factors[0, i] * before[i] - sides - around
                if i < HALO:
                    value = value * below
                if i >= HALO + SPAN:
                    value = value * above
                after[i] = value
            levels.append(after)
        for i in range(HALO, HALO + SPAN):
            for level in range(HALO + 1):
                kept.append((level, i - HALO, part, levels[level][i]))
            for n, (p, q) in enumerate(((0, 0), (0, 1), (1, 1), (1, 2), (2, 2), (2, 3))):
                products[n] = products[n] + levels[p][i] * levels[q][i]
    share = jnp.zeros((1, 128), F32)
    lane = iota((1, 128), 1)
    for n in range(6):
        inner = jnp.sum(jnp.sum(products[n], axis=0, keepdims=True), axis=1, keepdims=True)
        share = jnp.where(lane == n, jnp.broadcast_to(inner, (1, 128)), share)
    shares_out[...] = share

    for k in ROW_FAR_FIRST:
        to = lax.rem(row + k, NROW)
        copy_to(shares_out, shares_in.at[row], send_sem.at[6], recv_sem.at[6], brick, to).start()

    shares_in[row] = shares_out[...]

    for level, s, part, value in kept:
        fields[level, s, part, :] = value
    for level in range(HALO + 1):
        for s in range(SPAN):
            for c in range(3):
                for j in range(4):
                    line = fields[level, s, 4 * c + j : 4 * c + j + 1, :]
                    turned[level, c, s : s + 1, 128 * j : 128 * j + 128] = line

    await_copies(shares_in, NROW - 1, 6)
    share = shares_in[0]
    for k in range(1, NROW):
        share = share + shares_in[k]
    moment = [jnp.broadcast_to(share[:, n : n + 1], (8, 128)) for n in range(6)]
    matrix = [CENTRE * moment[n] + WIDTH * moment[n + 1] for n in range(5)]
    m00, m01, m02, m11, m12, m22 = matrix[0], matrix[1], matrix[2], matrix[2], matrix[3], matrix[4]
    l10 = m01 / m00
    l20 = m02 / m00
    d1 = m11 - l10 * m01
    e = m12 - l10 * m02
    l21 = e / d1
    d2 = m22 - l20 * m02 - l21 * e
    y1 = moment[1] - l10 * moment[0]
    y2 = moment[2] - l20 * moment[0] - l21 * y1
    w2 = y2 / d2
    w1 = y1 / d1 - l21 * w2
    w0 = moment[0] / m00 - l10 * w1 - l20 * w2
    r0 = 1.0 - CENTRE * w0
    r1 = -(WIDTH * w0 + CENTRE * w1)
    r2 = -(WIDTH * w1 + CENTRE * w2)
    r3 = -(WIDTH * w2)
    for c in range(3):
        for j in range(4):
            part = slice(128 * j, 128 * j + 128)
            v = [turned[level, c, :, part] for level in range(4)]
            displacement[c, :, part] = w0 * v[0] + w1 * v[1] + w2 * v[2]
            residual[c, :, part] = (r0 * v[0] + r1 * v[1]) + (r2 * v[2] + r3 * v[3])

    def await_sent(buffer, count, n):
        part = buffer.at[pl.ds(0, count)]
        copy_to(part, part, send_sem.at[n], recv_sem.at[n], brick_up, row).wait_send()

    await_sent(windows_in, NROW - 1, 0)
    await_sent(x_in, NX - 1, 1)
    await_sent(y_in, NY - 1, 2)
    await_sent(lines, NX - 1, 3)

    @pl.when(goes_up)
    def _():
        await_sent(lines, NX, 4)

    @pl.when(goes_down)
    def _():
        await_sent(lines, NX, 5)

    await_sent(shares_in, NROW - 1, 6)
    for copy in fluid_copies + stiff_copies:
        copy.wait_send()


def write_out(fluid, displacement, residual, fluid_far, displacement_far, residual_far, sem):
    copies = [
        pltpu.make_async_copy(near, far, sem.at[n])
        for n, (near, far) in enumerate(
            ((fluid, fluid_far), (displacement, displacement_far), (residual, residual_far))
        )
    ]
    for copy in copies:
        copy.start()
    for copy in copies:
        copy.wait()


def per_device(
    flow_state, point_cell, normals, rbf_weights, block_owner, block_start, stiff_diag, stiff_chord
):
    flow = flow_state.reshape(160, 128)
    weights = rbf_weights.reshape(NBLK * BP, 128)
    owner = block_owner.reshape(1, NBLK)
    start = block_start.reshape(1, NBLK)
    arrays = (flow, point_cell, normals, weights, owner, start, stiff_diag, stiff_chord)
    vmem = pl.BlockSpec(memory_space=pltpu.VMEM)
    far = pl.BlockSpec(memory_space=pltpu.HBM)
    dma = pltpu.SemaphoreType.DMA
    shapes = (
        jax.ShapeDtypeStruct((160, 128), F32),
        jax.ShapeDtypeStruct((3, SPAN, 512), F32),
        jax.ShapeDtypeStruct((3, SPAN, 512), F32),
    )
    results = pl.pallas_call(
        kernel,
        out_shape=shapes,
        in_specs=[far] * 8,
        out_specs=(vmem, vmem, vmem),
        scratch_shapes=[
            pltpu.VMEM((160, 128), F32),
            pltpu.VMEM((NBLK, BP), jnp.int32),
            pltpu.VMEM((3, NBLK, BP), F32),
            pltpu.VMEM((NBLK * BP, 128), BF16),
            pltpu.VMEM((1, NBLK), jnp.int32),
            pltpu.VMEM((1, NBLK), jnp.int32),
            pltpu.VMEM((SPAN, 512), F32),
            pltpu.VMEM((SPAN, 512), F32),
            pltpu.VMEM((8, 128), jnp.int32),
            pltpu.VMEM((8, 128), jnp.int32),
            pltpu.VMEM((3, NBLK, 128), F32),
            pltpu.VMEM((32, 128), F32),
            pltpu.VMEM((NROW, 8, 128), F32),
            pltpu.VMEM((NROW, 8, 128), F32),
            pltpu.VMEM((SPAN, LINE, 128), F32),
            pltpu.VMEM((NX, LINE, 128), F32),
            pltpu.VMEM((LINE, 128), F32),
            pltpu.VMEM((NY, LINE, 128), F32),
            pltpu.VMEM((ROWS, LINE, 128), F32),
            pltpu.VMEM((1, 128), F32),
            pltpu.VMEM((NROW, 1, 128), F32),
            pltpu.VMEM((2, 24, 128), F32),
            pltpu.VMEM((5, 8, 128), F32),
            pltpu.VMEM((5, 8, 128), F32),
            pltpu.VMEM((24, 128), F32),
            pltpu.VMEM((24, 128), F32),
            pltpu.VMEM((SPAN, 8, 128), F32),
            pltpu.VMEM((SPAN, 8, 128), F32),
            pltpu.VMEM((2, 2, 8, 128), F32),
            pltpu.VMEM((2, 2, 8, 128), F32),
            pltpu.VMEM((3, ROWS, 8, 128), F32),
            pltpu.VMEM((HALO + 1, SPAN, 16, 128), F32),
            pltpu.VMEM((HALO + 1, 3, SPAN, 512), F32),
            pltpu.SemaphoreType.REGULAR((4,)),
            dma((8,)),
            dma((7,)),
            dma((7,)),
            dma((12,)),
            dma((12,)),
            dma((4,)),
            dma((4,)),
        ],
        compiler_params=pltpu.CompilerParams(
            collective_id=0, has_side_effects=True, vmem_limit_bytes=16 * 1024 * 1024
        ),
        cost_estimate=pl.CostEstimate(flops=20_000_000, bytes_accessed=600_000, transcendentals=0),
        name="coupling_step",
    )(*[pltpu.with_memory_space_constraint(array, pltpu.HBM) for array in arrays])
    fluid_next, displacement, residual = pl.pallas_call(
        write_out,
        out_shape=shapes,
        in_specs=[vmem] * 3,
        out_specs=(far, far, far),
        scratch_shapes=[dma((3,))],
        compiler_params=pltpu.CompilerParams(vmem_limit_bytes=1024 * 1024),
        name="write_out",
    )(*[pltpu.with_memory_space_constraint(result, pltpu.VMEM) for result in results])
    return fluid_next.reshape(5, 4, 8, 128), displacement, residual


def solution(mesh):
    return jax.shard_map(
        per_device,
        mesh=mesh,
        in_specs=(
            P(None, "brick", "row", None),
            P(("brick", "row"), None),
            P(None, ("brick", "row"), None),
            P(("brick", "row"), None, None),
            P(("brick", "row"), None),
            P(("brick", "row")),
            P("row", None),
            P("row", None),
        ),
        out_specs=(P(None, "brick", "row", None), P(None, "row", None), P(None, "row", None)),
        check_vma=False,
    )
```
